32 devices in a mesh: gx: 8 (over z, y), gy: 4 (over x, core).
Axes of the slice: x: 2, y: 2, z: 4, core: 2. Of those that a mesh axis runs over, the one named last changes fastest.
Arguments:
- base_scores: float32 [12, 256, 64, 128], P(None, 'gx', 'gy'), may hold values from -6 to 6
- section_scores: float32 [12, 256, 64, 128], P(None, 'gx', 'gy'), may hold values from -6 to 6
- velocity: float32 [3, 256, 64, 128], P(None, 'gx', 'gy'), may hold values from -3 to 3
- diffusivity: float32 [256, 64, 128], P('gx', 'gy'), may hold values from 0.03 to 0.3
- w_first: bfloat16 [256, 12], replicated, may hold values from -1.75 to 1.75
- b_first: float32 [256], replicated, may hold values from -3 to 3
- w_second: bfloat16 [256, 256], replicated, may hold values from -0.375 to 0.375
- b_second: float32 [256], replicated, may hold values from -3 to 3
- w_third: bfloat16 [12, 256], replicated, may hold values from -0.375 to 0.375
- b_third: float32 [12], replicated, may hold values from -3 to 3
- loadings: bfloat16 [12, 300], replicated, may hold values from -0.375 to 0.375
- parcel_species: bfloat16 [1024, 300, 128], P(('gx', 'gy')), may hold values from -6 to 6
- parcel_owner: int32 [1024, 1], P(('gx', 'gy')), may hold values from 0 to 3; in each aligned block of 32 rows (0 to 31, 32 to 63, ...) at most 16 rows name the same one
- parcel_block: int32 [1024], P(('gx', 'gy')), may hold values from 0 to 31
Outputs:
- new_scores: float32 [12, 256, 64, 128], P(None, 'gx', 'gy')
The draws below stay inside these ranges and needn't reach their ends.
Inputs may be any that keep to these rules, and one draw needn't show every extreme that they name: `parcel_owner`: among the 32 parcel blocks of one device, no tile y index is named by more than 16 of them, and in every draw some device's blocks name one index exactly 16 times.
All inputs are finite; a program needn't handle non-finite values.
Results may differ from the reference program's by a relative error of at most 0.0003.
Values sent between devices are 32-bit elements; how exact they have to be, the bound alone decides.
No kernel may reach another device: no remote copies, remote signals or barrier semaphores. Data moves between devices by JAX's collectives and lax.ppermute only.
A program may use at most 64 MiB of HBM per device.

```python
import math
import jax
import jax.numpy as jnp
import numpy as np
from jax import lax

NPC = 12
SPEC = 300
HID = 256
LX = 32
LY = 16
NZ = 128
CB = 128
SB = 32
PB = 32
CAP = 16
NX = 256
NY = 64
PBLK = 1024
N_GX = 8
N_GY = 4


def touch_ends(array, stream_key, least, high):
    spot = [jax.random.randint(jax.random.fold_in(stream_key, axis), (), 0, length) for axis, length in enumerate(array.shape)]
    main_axis = array.shape.index(max(array.shape))
    beside = spot[:main_axis] + [(spot[main_axis] + 1) % array.shape[main_axis]] + spot[main_axis + 1:]
    return array.at[tuple(spot)].set(least).at[tuple(beside)].set(high)


def shard_levels(rng, dims, cuts, low, high):
    def one(dim, blocks):
        draws = jax.random.uniform(jax.random.fold_in(jax.random.fold_in(rng, 6), dim), (blocks,), jnp.float32, low / len(cuts), high / len(cuts))
        return jnp.repeat(jnp.exp(draws), dims[dim] // blocks).reshape((-1,) + (1,) * (len(dims) - dim - 1))

    loudness = one(*cuts[0])
    for cut in cuts[1:]:
        loudness = loudness * one(*cut)
    return loudness


def routed_block(key, own, number, rows, amount, top, most, lean):
    order = jax.random.permutation(key, amount)
    crowded, common = load_shares(amount, rows * top, most, lean, True), load_shares(amount, rows * top, most, lean, False)
    places = jnp.arange(amount)

    def named(tallies, turn):
        used = int((tallies > 0).sum())
        fixed = max(1, used // 4)
        moved = fixed + (places - fixed + turn * (used - fixed)) % max(1, amount - fixed)
        return jnp.zeros((amount,), jnp.int32).at[order[jnp.where(places < fixed, places, moved)]].set(jnp.asarray(tallies, jnp.int32))

    tallies = jnp.where(number % 4 == 0, named(crowded, number // 4), named(common, number - number // 4 - 1))
    mixed = jax.random.permutation(jax.random.fold_in(own, 3), amount)
    giver, sink = mixed[0:amount // 2 * 2:2], mixed[1:amount // 2 * 2:2]
    slack = jnp.minimum(tallies[giver] - 1, most - tallies[sink]) // 2
    slack = jnp.where((giver == order[0]) | (sink == order[0]) | (tallies[sink] == 0), 0, jnp.maximum(slack, 0))
    moved = jax.random.randint(jax.random.fold_in(own, 4), (amount // 2,), 0, 1 << 20) % (slack + 1)
    tallies = tallies.at[giver].add(-moved).at[sink].add(moved)
    labels = jnp.searchsorted(jnp.cumsum(tallies), jnp.arange(rows * top), side="right").astype(jnp.int32)
    table = labels.reshape(top, rows).T
    table = table[jax.random.permutation(jax.random.fold_in(own, 1), rows)]
    turn = jax.random.randint(jax.random.fold_in(own, 2), (rows, 1), 0, top)
    return jnp.take_along_axis(table, (jnp.arange(top)[None, :] + turn) % top, axis=1)


def load_shares(amount, total, most, lean, full):
    loads = [(1 << 20) // math.isqrt(standing ** lean) + 1 for standing in range(1, amount + 1)]
    largest = most if full else min(most, max(-(-total // amount), total * loads[0] // sum(loads)))
    least = 1 if total - largest >= amount - 1 else 0
    holding, rest = [largest] + [least] * (amount - 1), total - largest - least * (amount - 1)
    while rest > 0:
        movable = [i for i in range(1, amount) if holding[i] < largest] or [i for i in range(1, amount) if holding[i] < most]
        whole, budget = sum([loads[i] for i in movable]), rest
        for i in movable:
            more = min(most - holding[i], max(1, budget * loads[i] // whole), rest)
            holding[i] = holding[i] + more
            rest = rest - more
    return np.array(holding)


def normal_values(key, shape, scale, most, cuts=(), kind=jnp.bfloat16):
    values = scale * jax.random.normal(key, shape, jnp.float32)
    if cuts:
        values = values * shard_levels(key, shape, cuts, -0.22, 0.18)
    return jnp.clip(values, -most, most).astype(kind)


def setup_inputs(seed: int = 0) -> dict:
    keys = jax.random.split(jax.random.key(seed), 15)
    base_scores = normal_values(keys[0], (NPC, NX, NY, NZ), 1.0, 6.0, ((1, 8), (2, 4)), jnp.float32)
    section_scores = normal_values(keys[1], (NPC, NX, NY, NZ), 1.0, 6.0, ((1, 8), (2, 4)), jnp.float32)
    velocity = normal_values(keys[2], (3, NX, NY, NZ), 0.6, 3.0, ((1, 8), (2, 4)), jnp.float32)
    diffusivity = jnp.clip(jnp.exp(math.log(0.3) - 2.3025852 * jax.random.uniform(keys[3], (NX, NY, NZ), jnp.float32) ** shard_levels(keys[3], (NX, NY, NZ), ((0, 8), (1, 4)), -0.2, 0.2)), 0.03, 0.3)
    w_first = normal_values(keys[4], (HID, NPC), NPC ** -0.5, 1.75)
    b_first = normal_values(keys[5], (HID,), 0.5, 3.0, (), jnp.float32)
    w_second = normal_values(keys[6], (HID, HID), HID ** -0.5, 0.375)
    b_second = normal_values(keys[7], (HID,), 0.5, 3.0, (), jnp.float32)
    w_third = normal_values(keys[8], (NPC, HID), HID ** -0.5, 0.375)
    b_third = normal_values(keys[9], (NPC,), 0.5, 3.0, (), jnp.float32)
    loadings = normal_values(keys[10], (NPC, SPEC), SPEC ** -0.5, 0.375)
    parcel_species = normal_values(keys[11], (PBLK, SPEC, CB), 1.0, 6.0, ((0, 32),))
    parcel_owner_keys = jax.random.split(jax.random.fold_in(keys[12], 1), PBLK // PB)
    parcel_owner_turns = jax.random.permutation(jax.random.fold_in(keys[12], 3), PBLK // PB)
    parcel_owner = jax.vmap(lambda own, number: routed_block(jax.random.fold_in(keys[12], 2), own, number, PB, N_GY, 1, CAP, 2))(parcel_owner_keys, parcel_owner_turns).reshape((PBLK, 1))
    parcel_block = touch_ends(jax.random.randint(keys[13], (PBLK,), 0, SB), jax.random.fold_in(keys[13], 1), 0, SB - 1).astype(jnp.int32)
    return dict(base_scores=base_scores, section_scores=section_scores, velocity=velocity, diffusivity=diffusivity, w_first=w_first, b_first=b_first, w_second=w_second, b_second=b_second, w_third=w_third, b_third=b_third, loadings=loadings, parcel_species=parcel_species, parcel_owner=parcel_owner, parcel_block=parcel_block)


dt_step = 0.25


def regress(block, w_first, b_first, w_second, b_second, w_third, b_third):
    inputs = block.astype(jnp.bfloat16)
    first = jnp.tanh(jnp.dot(w_first, inputs, preferred_element_type=jnp.float32) + b_first[:, None]).astype(jnp.bfloat16)
    second = jnp.tanh(jnp.dot(w_second, first, preferred_element_type=jnp.float32) + b_second[:, None]).astype(jnp.bfloat16)
    return jnp.dot(w_third, second, preferred_element_type=jnp.float32) + b_third[:, None]


def sources(flat, weights):
    comps, count = flat.shape
    width = math.gcd(count, 4096)
    blocks = flat.reshape(comps, count // width, width).transpose(1, 0, 2)
    result = lax.map(lambda piece: regress(piece, *weights), blocks)
    return result.transpose(1, 0, 2).reshape(comps, count)


def transport_rate(center, plus_x, minus_x, plus_y, minus_y, plus_z, minus_z, velocity, diffusivity):
    drift = velocity[0] * (plus_x - minus_x) + velocity[1] * (plus_y - minus_y) + velocity[2] * (plus_z - minus_z)
    spread = plus_x + minus_x + plus_y + minus_y + plus_z + minus_z - 6.0 * center
    return diffusivity * spread - 0.5 * drift


def reference(base_scores, section_scores, velocity, diffusivity, w_first, b_first, w_second, b_second, w_third, b_third, loadings, parcel_species, parcel_owner, parcel_block):
    def one_score(field):
        padded = jnp.pad(field, 1)
        return transport_rate(field, padded[2:, 1:-1, 1:-1], padded[:-2, 1:-1, 1:-1], padded[1:-1, 2:, 1:-1], padded[1:-1, :-2, 1:-1], padded[1:-1, 1:-1, 2:], padded[1:-1, 1:-1, :-2], velocity, diffusivity)

    transport = lax.map(one_score, section_scores)
    weights = (w_first, b_first, w_second, b_second, w_third, b_third)
    chemistry = sources(section_scores.reshape(NPC, -1), weights).reshape(section_scores.shape)
    total = PB * N_GX * N_GY
    grouped = parcel_species.reshape(total // PB, PB, SPEC, CB)
    load_wide = loadings.astype(jnp.float32)
    projected = lax.map(lambda group: jnp.einsum("ks,psc->pkc", load_wide, group.astype(jnp.float32), precision=lax.Precision.HIGHEST).astype(jnp.bfloat16), grouped)
    projected = lax.optimization_barrier(projected)
    projected = projected.reshape(total, NPC * CB).astype(jnp.float32)
    source_row = (jnp.arange(total, dtype=jnp.int32) // (PB * N_GY)).astype(jnp.int32)
    segment = ((source_row * N_GY + parcel_owner[:, 0]) * SB + parcel_block).astype(jnp.int32)
    deposit = jax.ops.segment_sum(projected, segment, num_segments=N_GX * N_GY * SB)
    deposit = deposit.reshape(N_GX, N_GY, SB, NPC, CB).transpose(3, 0, 1, 2, 4).reshape(NPC, N_GX, N_GY, SB * CB)
    cells = LX * LY * NZ
    deposit = jnp.pad(deposit, ((0, 0), (0, 0), (0, 0), (0, cells - SB * CB)))
    spray = deposit.reshape(NPC, N_GX, N_GY, LX, LY, NZ).transpose(0, 1, 3, 2, 4, 5).reshape(NPC, N_GX * LX, N_GY * LY, NZ)
    rate = transport + chemistry + spray
    return 0.75 * base_scores + 0.25 * (section_scores + dt_step * rate)
```

```python
import math

import jax
import jax.numpy as jnp
from jax import lax
from jax.sharding import PartitionSpec as P

SB = 32


dt_step = 0.25


def with_halo(block, sides, width):
    for axis, dim in sides:
        count = lax.axis_size(axis)
        forward = [(i, i + 1) for i in range(count - 1)]
        backward = [(target, source) for source, target in forward]
        low = lax.ppermute(
            lax.slice_in_dim(block, block.shape[dim] - width, None, axis=dim), axis, forward
        )
        high = lax.ppermute(lax.slice_in_dim(block, 0, width, axis=dim), axis, backward)
        block = jnp.concatenate([low, block, high], axis=dim)
    return block


def regress(block, w_first, b_first, w_second, b_second, w_third, b_third):
    inputs = block.astype(jnp.bfloat16)
    first = jnp.tanh(
        jnp.dot(w_first, inputs, preferred_element_type=jnp.float32) + b_first[:, None]
    ).astype(jnp.bfloat16)
    second = jnp.tanh(
        jnp.dot(w_second, first, preferred_element_type=jnp.float32) + b_second[:, None]
    ).astype(jnp.bfloat16)
    return jnp.dot(w_third, second, preferred_element_type=jnp.float32) + b_third[:, None]


def sources(flat, weights):
    comps, count = flat.shape
    width = math.gcd(count, 4096)
    blocks = flat.reshape(comps, count // width, width).transpose(1, 0, 2)
    result = lax.map(lambda piece: regress(piece, *weights), blocks)
    return result.transpose(1, 0, 2).reshape(comps, count)


def transport_rate(
    center, plus_x, minus_x, plus_y, minus_y, plus_z, minus_z, velocity, diffusivity
):
    drift = (
        velocity[0] * (plus_x - minus_x)
        + velocity[1] * (plus_y - minus_y)
        + velocity[2] * (plus_z - minus_z)
    )
    spread = plus_x + minus_x + plus_y + minus_y + plus_z + minus_z - 6.0 * center
    return diffusivity * spread - 0.5 * drift


def shards(
    base_scores,
    section_scores,
    velocity,
    diffusivity,
    w_first,
    b_first,
    w_second,
    b_second,
    w_third,
    b_third,
    loadings,
    parcel_species,
    parcel_owner,
    parcel_block,
):
    comps, rows_x, rows_y, depth = section_scores.shape
    padded = with_halo(section_scores, (("gx", 1), ("gy", 2)), 1)
    plus_x = padded[:, 2:, 1:-1]
    minus_x = padded[:, :-2, 1:-1]
    plus_y = padded[:, 1:-1, 2:]
    minus_y = padded[:, 1:-1, :-2]
    along_z = jnp.pad(section_scores, ((0, 0), (0, 0), (0, 0), (1, 1)))
    transport = transport_rate(
        section_scores,
        plus_x,
        minus_x,
        plus_y,
        minus_y,
        along_z[..., 2:],
        along_z[..., :-2],
        velocity,
        diffusivity,
    )
    weights = (w_first, b_first, w_second, b_second, w_third, b_third)
    chemistry = sources(section_scores.reshape(comps, -1), weights).reshape(section_scores.shape)
    blocks_here = parcel_species.shape[0]
    block_cells = parcel_species.shape[2]
    projected = jnp.einsum(
        "ks,psc->pkc", loadings, parcel_species, preferred_element_type=jnp.float32
    ).astype(jnp.bfloat16)
    projected = projected.reshape(blocks_here, comps * block_cells)
    owner = parcel_owner[:, 0]
    tiles_y = lax.axis_size("gy")
    capacity = max(2, 2 * blocks_here // tiles_y)
    places = jnp.arange(blocks_here, dtype=jnp.int32)
    earlier = (owner[None, :] == owner[:, None]) & (places[None, :] < places[:, None])
    ranks = jnp.sum(earlier.astype(jnp.int32), axis=1)
    slot_ids = owner * capacity + ranks
    chosen = slot_ids[None, :] == jnp.arange(tiles_y * capacity, dtype=jnp.int32)[:, None]
    values = jnp.dot(chosen.astype(jnp.bfloat16), projected, preferred_element_type=jnp.float32)
    tags = jnp.sum(jnp.where(chosen, parcel_block[None, :] + 1, 0), axis=1)
    got_values, got_tags = (
        lax.all_to_all(values, "gy", split_axis=0, concat_axis=0, tiled=True),
        lax.all_to_all(tags, "gy", split_axis=0, concat_axis=0, tiled=True),
    )
    placing = (got_tags[None, :] - 1 == jnp.arange(SB, dtype=jnp.int32)[:, None]).astype(
        jnp.float32
    )
    mine = jnp.dot(
        placing, got_values, preferred_element_type=jnp.float32, precision=lax.Precision.HIGHEST
    )
    spray = mine.reshape(SB, comps, block_cells).transpose(1, 0, 2).reshape(comps, SB * block_cells)
    cells = rows_x * rows_y * depth
    spray = jnp.pad(spray, ((0, 0), (0, cells - SB * block_cells))).reshape(section_scores.shape)
    rate = transport + chemistry + spray
    return 0.75 * base_scores + 0.25 * (section_scores + dt_step * rate)


def solution(mesh):
    placed = (
        P(None, "gx", "gy", None),
        P(None, "gx", "gy", None),
        P(None, "gx", "gy", None),
        P("gx", "gy", None),
        P(),
        P(),
        P(),
        P(),
        P(),
        P(),
        P(),
        P(("gx", "gy"), None, None),
        P(("gx", "gy"), None),
        P(("gx", "gy")),
    )
    return jax.shard_map(
        shards, mesh=mesh, in_specs=placed, out_specs=P(None, "gx", "gy", None), check_vma=False
    )
```

```python
import functools

import jax
import jax.numpy as jnp
from jax import lax
from jax.experimental import pallas as pl
from jax.experimental.pallas import tpu as pltpu
from jax.sharding import PartitionSpec as P

SB = 32

dt_step = 0.25
keep_base = 0.75
keep_section = 0.25
scale = keep_section * dt_step

TILE = 256
f32, bf16 = jnp.float32, jnp.bfloat16


def bias_column(row, width):
    return jnp.transpose(jnp.broadcast_to(row, (width, row.shape[1])))


def prepare_weights(w1t, b1, w2, b2, w3, b3, w1_s, b2_s, w3_s, b3_s):
    comps, hidden = w1t.shape
    bias = b1[...]
    high = bias.astype(bf16).astype(f32)
    middle = (bias - high).astype(bf16).astype(f32)
    low = (bias - high - middle).astype(bf16).astype(f32)
    rows = jnp.concatenate(
        [w1t[...].astype(f32), high, middle, low]
        + [jnp.zeros((128 - comps - 3, hidden), f32)],
        axis=0,
    )
    first = jnp.transpose(rows).astype(bf16)
    w1_s[...] = jnp.concatenate(
        [first, jnp.zeros((hidden, TILE - 128), bf16)], axis=1
    )
    b2_s[...] = bias_column(b2[...], 128)
    w3_s[...] = jnp.concatenate(
        [w3[...].astype(f32), jnp.zeros((16 - comps, hidden), f32)], axis=0
    ).astype(bf16)
    row = jnp.concatenate([b3[...], jnp.zeros((1, 128 - comps), f32)], axis=1)
    b3_s[...] = bias_column(row, 128)[:16]


def regression_stages(
    cells, comps, planes, rows_y, w1_s, w2, b2_s, w3_s, b3_s, first_s, second_s, accs, put
):
    total = cells.shape[0] // comps
    across = TILE // 128
    tiles = rows_y // across
    ones = jnp.ones((16 - comps, 128), f32)
    empty = jnp.zeros((TILE - 16, TILE), bf16)
    first_acc, second_acc, third_acc = accs

    def widen(column):
        return jnp.concatenate([column] * across, axis=1)

    def layer1(row0, slot, tile):
        mxu = tile % 2
        parts = []
        for k in range(across):
            part = cells[pl.ds(row0 + tile * across + k, comps, stride=total), :]
            parts.append(jnp.concatenate([part, ones], axis=0).astype(bf16))
        block = jnp.concatenate([jnp.concatenate(parts, axis=1), empty], axis=0)
        pltpu.matmul_push_rhs(block, 0, mxu)
        pltpu.matmul_acc_lhs(first_acc[mxu], w1_s[...], load_staged_rhs=0)

        def finish():
            out = pltpu.matmul_pop(first_acc[mxu])
            first_s[slot][:, pl.ds(tile * TILE, TILE)] = jnp.tanh(out).astype(bf16)

        return finish

    def layer2(slot, tile):
        mxu = tile % 2
        pltpu.matmul_push_rhs(first_s[slot][:, pl.ds(tile * TILE, TILE)], 1, mxu)
        pltpu.matmul_acc_lhs(second_acc[mxu], w2[...], load_staged_rhs=1)

        def finish():
            out = pltpu.matmul_pop(second_acc[mxu]) + widen(b2_s[...])
            second_s[slot][:, pl.ds(tile * TILE, TILE)] = jnp.tanh(out).astype(bf16)

        return finish

    def layer3(plane, slot, tile):
        mxu = tile % 2
        pltpu.matmul_push_rhs(second_s[slot][:, pl.ds(tile * TILE, TILE)], 0, mxu)
        pltpu.matmul_acc_lhs(third_acc[mxu], w3_s[...], load_staged_rhs=0)

        def finish():
            out = pltpu.matmul_pop(third_acc[mxu]) + widen(b3_s[...])
            for k in range(across):
                put(plane, tile * across + k, out[:comps, k * 128 : (k + 1) * 128])

        return finish

    def stage(one=None, two=None, three=None, beside=None):
        late = []
        for pair in range(0, tiles, 2):
            now = range(pair, min(pair + 2, tiles))
            ready = []
            if one is not None:
                ready += [layer1(*one, t) for t in now]
            for finish in late:
                finish()
            late = []
            if three is not None:
                ready += [layer3(*three, t) for t in now]
            if two is not None:
                late = [layer2(two, t) for t in now]
            for finish in ready:
                finish()
            if beside is not None:
                beside(pair // 2, (tiles + 1) // 2)
        for finish in late:
            finish()

    return stage


def accumulators(body):
    spaces = []
    for rows in (TILE, TILE, 16):
        spaces += [pltpu.ACC(mxu_id=m)((rows, TILE), f32) for m in range(2)]

    def inner(a0, a1, b0, b1, c0, c1):
        body(((a0, a1), (b0, b1), (c0, c1)))

    pl.run_scoped(inner, *spaces)


def chemistry_kernel(
    section, w1t, b1, w2, b2, w3, b3, out, cells, held, w1_s, b2_s, w3_s, b3_s, first_0, first_1, second_0, second_1, load_sem, store_sem,
    *, start, planes,
):
    first_s, second_s = (first_0, first_1), (second_0, second_1)
    comps, _, rows_y, _ = section.shape

    def load(i):
        return pltpu.make_async_copy(
            section.at[:, pl.ds(start + i, 1)], cells.at[:, pl.ds(i, 1)], load_sem.at[i]
        )

    def store(i):
        return pltpu.make_async_copy(
            held.at[:, pl.ds(i, 1)], out.at[:, pl.ds(i, 1)], store_sem.at[i]
        )

    for i in range(planes):
        load(i).start()
    prepare_weights(w1t, b1, w2, b2, w3, b3, w1_s, b2_s, w3_s, b3_s)
    flat = cells.reshape(comps * planes * rows_y, 128)
    held_flat = held.reshape(comps * planes * rows_y, 128)

    def put(plane, row, value):
        held_flat[pl.ds(plane * rows_y + row, comps, stride=planes * rows_y), :] = value

    def body(accs):
        stage = regression_stages(
            flat, comps, planes, rows_y, w1_s, w2, b2_s, w3_s, b3_s, first_s, second_s, accs, put
        )
        load(0).wait()
        stage(one=(0, 0))
        load(1).wait()
        stage(one=(rows_y, 1), two=0)

        def step(pair, carry):
            for odd in range(2):
                i = 2 * pair + odd
                load(i).wait()
                stage(one=(i * rows_y, odd), two=1 - odd, three=(i - 2, odd))
                store(i - 2).start()
            return carry

        lax.fori_loop(1, planes // 2, step, 0)
        last = planes - 1
        stage(two=last % 2, three=(last - 1, (last - 1) % 2))
        store(last - 1).start()
        stage(three=(last, last % 2))
        store(last).start()

    accumulators(body)
    for i in range(planes):
        store(i).wait()


def section_kernel(
    section, base, velocity, diffusivity, chem_in, from_low_x, from_high_x, *refs, planes, places
):
    parts = refs[: len(places)]
    (
        w1t, b1, w2, b2, w3, b3, out,
        cells, base_s, vel_s, diff_s, chem_s, out_s, w1_s, b2_s, w3_s, b3_s,
        first_0, first_1, second_0, second_1, place_s,
        cell_sem, base_sem, vel_sem, diff_sem, chem_sem, edge_sem, store_sem,
    ) = refs[len(places) : len(places) + 29]
    held_parts = refs[len(places) + 29 : -1]
    part_sem = refs[-1]
    first_s, second_s = (first_0, first_1), (second_0, second_1)
    comps, all_planes, rows_y, depth = section.shape
    stride = (all_planes + 2) * rows_y
    slots = parts[0].shape[1] - places[0]
    count = len(places) * slots
    low_y, high_y = held_parts[1], held_parts[2]

    def load_cells(x):
        return pltpu.make_async_copy(
            section.at[:, pl.ds(x, 1)], cells.at[:, pl.ds(x + 1, 1)], cell_sem.at[x]
        )

    def load_rest(x):
        one = pl.ds(x, 1)
        return [
            pltpu.make_async_copy(base.at[:, one], base_s.at[:, one], base_sem.at[x]),
            pltpu.make_async_copy(velocity.at[:, one], vel_s.at[:, one], vel_sem.at[x]),
            pltpu.make_async_copy(diffusivity.at[one], diff_s.at[one], diff_sem.at[x]),
        ]

    def load_chem(x):
        return pltpu.make_async_copy(
            chem_in.at[:, pl.ds(x - planes, 1)], chem_s.at[:, pl.ds(x, 1)], chem_sem.at[x - planes]
        )

    def store(x):
        return pltpu.make_async_copy(
            out_s.at[:, pl.ds(x, 1)], out.at[:, pl.ds(x, 1)], store_sem.at[x]
        )

    edges = [
        pltpu.make_async_copy(from_low_x, cells.at[:, 0], edge_sem.at[0]),
        pltpu.make_async_copy(from_high_x, cells.at[:, all_planes + 1], edge_sem.at[1]),
    ]
    coming = [
        pltpu.make_async_copy(part, held, part_sem.at[k])
        for k, (part, held) in enumerate(zip(parts, held_parts))
    ]
    spray_planes = SB // rows_y

    load_cells(0).start()
    load_cells(planes - 1).start()
    load_cells(planes).start()
    load_cells(planes + 1).start()
    for copy in coming:
        copy.start()
    for x in range(spray_planes):
        load_rest(x)[0].start()
    for x in range(planes):
        if x + 1 < planes - 1:
            load_cells(x + 1).start()
        if planes + x + 2 < all_planes:
            load_cells(planes + x + 2).start()
        load_chem(planes + x).start()
        for copy in load_rest(planes + x):
            copy.start()
        for copy in load_rest(x)[x < spray_planes :]:
            copy.start()
        if x == 1:
            for copy in edges:
                copy.start()
    prepare_weights(w1t, b1, w2, b2, w3, b3, w1_s, b2_s, w3_s, b3_s)

    flat = cells.reshape(comps * stride, 128)
    chem_flat = chem_s.reshape(comps * all_planes * rows_y, 128)

    def put(plane, row, value):
        chem_flat[pl.ds(plane * rows_y + row, comps, stride=all_planes * rows_y), :] = value

    row_id = lax.broadcasted_iota(jnp.int32, (rows_y, depth), 0)
    lane_id = lax.broadcasted_iota(jnp.int32, (rows_y, depth), 1)

    def coefficients(x):
        spread = scale * diff_s[x]
        half = [(0.5 * scale) * vel_s[d, x] for d in range(3)]
        up = [spread - h for h in half]
        down = [spread + h for h in half]
        up[2] = jnp.where(lane_id == depth - 1, 0.0, up[2])
        down[2] = jnp.where(lane_id == 0, 0.0, down[2])
        return up, down, keep_section - 6.0 * spread

    def combine(x, comp, up, down, middle):
        center = cells[comp, x + 1]
        above_y = jnp.broadcast_to(high_y[comp, pl.ds(x, 1), :], (rows_y, depth))
        below_y = jnp.broadcast_to(low_y[comp, pl.ds(x, 1), :], (rows_y, depth))
        plus_y = jnp.where(row_id == rows_y - 1, above_y, pltpu.roll(center, rows_y - 1, 0))
        minus_y = jnp.where(row_id == 0, below_y, pltpu.roll(center, 1, 0))
        total = keep_base * base_s[comp, x] + middle * center
        total += up[0] * cells[comp, x + 2] + down[0] * cells[comp, x]
        total += up[1] * plus_y + down[1] * minus_y
        total += up[2] * pltpu.roll(center, depth - 1, 1) + down[2] * pltpu.roll(center, 1, 1)
        out_s[comp, x] = total + scale * chem_s[comp, x]

    def update(x, part=0, pieces=1):
        up, down, middle = coefficients(x)
        for comp in range(part * comps // pieces, (part + 1) * comps // pieces):
            combine(x, comp, up, down, middle)

    def deposit(first_acc):
        tags = jnp.concatenate(
            [held[comps, pl.ds(row, slots)] for held, row in zip(held_parts, places)], axis=0
        )
        lanes = lax.broadcasted_iota(jnp.int32, tags.shape, 1).astype(f32)
        chosen = jnp.transpose((tags - 1.0 == lanes).astype(f32))
        place_s[...] = jnp.zeros(place_s.shape, bf16)
        place_s[:SB, :count] = chosen[:SB].astype(bf16)
        for comp in range(0, comps, 2):
            mxu = (comp // 2) % 2
            pair = [
                jnp.concatenate(
                    [held[comp + k, pl.ds(row, slots)] for held, row in zip(held_parts, places)],
                    axis=0,
                )
                for k in range(2)
            ]
            block = jnp.concatenate(pair, axis=1).astype(bf16)
            block = jnp.concatenate([block, jnp.zeros((TILE - count, TILE), bf16)], axis=0)
            pltpu.matmul_push_rhs(block, 0, mxu)
            pltpu.matmul_acc_lhs(first_acc[mxu], place_s[...], load_staged_rhs=0)
            mine = pltpu.matmul_pop(first_acc[mxu])[:SB]
            for k in range(2):
                piece = mine[:, k * 128 : (k + 1) * 128].reshape(spray_planes, rows_y, depth)
                base_s[comp + k, :spray_planes] += (scale / keep_base) * piece

    def body(accs):
        stage = regression_stages(
            flat, comps, planes, rows_y, w1_s, w2, b2_s, w3_s, b3_s, first_s, second_s, accs, put
        )

        def far_ready(i):
            @pl.when(i < planes - 1)
            def _():
                load_cells(planes + i + 1).wait()

            load_chem(planes + i).wait()
            for copy in load_rest(planes + i):
                copy.wait()

        def near_ready(i):
            for copy in load_rest(i)[1:]:
                copy.wait()

            @pl.when(i >= spray_planes)
            def _():
                load_rest(i)[0].wait()

        def run(i, near, **layers):
            far_ready(i)
            if near is not None:
                near_ready(near)

            def beside(part, pieces):
                if near is None:
                    update(planes + i, part, pieces)
                elif part < pieces // 2:
                    update(planes + i, part, pieces // 2)
                else:
                    update(near, part - pieces // 2, pieces - pieces // 2)

            stage(beside=beside, **layers)
            store(planes + i).start()
            if near is not None:
                store(near).start()

        load_cells(0).wait()
        load_cells(planes - 1).wait()
        load_cells(planes).wait()
        for copy in coming:
            copy.wait()
        for x in range(spray_planes):
            load_rest(x)[0].wait()
        deposit(accs[0])
        for copy in edges:
            copy.wait()

        run(0, None, one=(rows_y, 0))
        load_cells(1).wait()
        run(1, None, one=(2 * rows_y, 1), two=0)
        load_cells(2).wait()
        run(2, None, one=(3 * rows_y, 0), two=1, three=(0, 0))
        load_cells(3).wait()
        run(3, 0, one=(4 * rows_y, 1), two=0, three=(1, 1))

        def step(pair, carry):
            for odd in range(2):
                i = 2 * pair + odd

                @pl.when(i < planes - 1)
                def _():
                    load_cells(i).wait()

                run(i, i - 3, one=((i + 1) * rows_y, odd), two=1 - odd, three=(i - 2, odd))
            return carry

        lax.fori_loop(2, planes // 2, step, 0)
        last = planes - 1
        near_ready(last - 2)
        stage(
            two=last % 2,
            three=(last - 1, (last - 1) % 2),
            beside=functools.partial(update, last - 2),
        )
        store(last - 2).start()
        near_ready(last - 1)
        stage(three=(last, last % 2), beside=functools.partial(update, last - 1))
        store(last - 1).start()
        near_ready(last)
        update(last)
        store(last).start()

    accumulators(body)
    for x in range(all_planes):
        store(x).wait()


def faces_kernel(owner, block, projected, section, low_x, high_x, *refs, shifts):
    sends, (lower, upper, sems) = refs[:-3], refs[-3:]
    comps, planes, rows_y, depth = section.shape
    edge = lower.shape[2]
    count = projected.shape[1]
    tiles_y = len(shifts)
    capacity = sends[0].shape[1]
    me = lax.axis_index("gy")
    copies = [
        pltpu.make_async_copy(section.at[:, :, pl.ds(0, edge)], lower, sems.at[0]),
        pltpu.make_async_copy(section.at[:, :, pl.ds(rows_y - edge, edge)], upper, sems.at[1]),
        pltpu.make_async_copy(section.at[:, 0], low_x, sems.at[2]),
        pltpu.make_async_copy(section.at[:, planes - 1], high_x, sems.at[3]),
    ]
    for copy in copies:
        copy.start()
    own = owner[...]
    some = -(-tiles_y // 8) * 8
    hits = (lax.broadcasted_iota(jnp.int32, (some, count), 0) == own).astype(f32)
    before = lax.broadcasted_iota(jnp.int32, (count, count), 0) < lax.broadcasted_iota(
        jnp.int32, (count, count), 1
    )
    counts = jnp.dot(
        hits.astype(bf16), before.astype(f32).astype(bf16), preferred_element_type=f32
    )
    rank = jnp.sum(counts * hits, axis=0, keepdims=True).astype(jnp.int32)
    order = jnp.zeros_like(own)
    for k, shift in enumerate(shifts):
        order = jnp.where(own == lax.rem(me + shift, tiles_y), k, order)
    slot = order * capacity + rank
    chosen = lax.broadcasted_iota(jnp.int32, (tiles_y * capacity, count), 0) == slot
    numbers = jnp.sum(
        jnp.where(chosen, (block[...] + 1).astype(f32), 0.0), axis=1, keepdims=True
    )
    numbers = jnp.broadcast_to(numbers, (tiles_y * capacity, depth))
    picked = chosen.astype(f32).astype(bf16)

    def put(comp, value):
        for k, send in enumerate(sends):
            rows = pl.ds(send.shape[1] - capacity, capacity)
            send[comp, rows] = value[k * capacity : (k + 1) * capacity]

    for comp in range(comps):
        put(comp, jnp.dot(picked, projected[comp], preferred_element_type=f32))
    put(comps, numbers)
    for copy in copies:
        copy.wait()
    for send, held, row, last in (
        (sends[1], upper, edge - 1, me == tiles_y - 1),
        (sends[2], lower, 0, me == 0),
    ):
        lines = held.reshape(comps * planes * edge, depth)
        layer = lines[pl.ds(row, comps * planes, stride=edge), :]
        layer = jnp.where(last, 0.0, layer)
        for comp in range(comps):
            send[comp, pl.ds(0, planes)] = layer[comp * planes : (comp + 1) * planes]
        send[comps, pl.ds(0, planes)] = jnp.zeros((planes, depth), f32)


def shards(
    base_scores,
    section_scores,
    velocity,
    diffusivity,
    w_first,
    b_first,
    w_second,
    b_second,
    w_third,
    b_third,
    loadings,
    parcel_species,
    parcel_owner,
    parcel_block,
):
    comps, rows_x, rows_y, depth = section_scores.shape
    hidden = w_second.shape[0]
    blocks_here = parcel_species.shape[0]
    tiles_y = lax.axis_size("gy")
    capacity = max(2, 2 * blocks_here // tiles_y)
    planes = rows_x // 2
    rest = rows_x - planes
    whole = pl.BlockSpec(memory_space=pltpu.VMEM)
    anywhere = pl.BlockSpec(memory_space=pltpu.HBM)
    sems = pltpu.SemaphoreType.DMA
    params = pltpu.CompilerParams(vmem_limit_bytes=60 * 2**20)

    projected = jnp.einsum(
        "ks,psc->kpc", loadings, parcel_species, preferred_element_type=f32
    ).astype(bf16)
    shifts = [0, 1, tiles_y - 1] + list(range(2, tiles_y - 1))
    faces = [0, rows_x, rows_x] + [0] * (tiles_y - 3)
    face_x = jax.ShapeDtypeStruct((comps, rows_y, depth), f32)
    low_x, high_x, *sends = pl.pallas_call(
        functools.partial(faces_kernel, shifts=shifts),
        in_specs=[whole] * 3 + [anywhere],
        out_specs=[whole] * (2 + tiles_y),
        out_shape=[face_x] * 2
        + [jax.ShapeDtypeStruct((comps + 1, face + capacity, depth), f32) for face in faces],
        scratch_shapes=[pltpu.VMEM((comps, rows_x, 8, depth), f32)] * 2 + [sems((4,))],
        compiler_params=params,
    )(parcel_owner.reshape(1, -1), parcel_block.reshape(1, -1), projected, section_scores)

    tiles_x = lax.axis_size("gx")
    forward = [(i, i + 1) for i in range(tiles_x - 1)]
    backward = [(target, source) for source, target in forward]
    from_low_x = lax.ppermute(high_x, "gx", forward)
    from_high_x = lax.ppermute(low_x, "gx", backward)
    parts = [sends[0]] + [
        lax.ppermute(send, "gy", [(i, (i + shift) % tiles_y) for i in range(tiles_y)])
        for send, shift in zip(sends[1:], shifts[1:])
    ]

    weights = (
        w_first.T,
        b_first.reshape(1, -1),
        w_second,
        b_second.reshape(1, -1),
        w_third,
        b_third.reshape(1, -1),
    )
    prepared = [
        pltpu.VMEM((hidden, TILE), bf16),
        pltpu.VMEM((hidden, 128), f32),
        pltpu.VMEM((16, hidden), bf16),
        pltpu.VMEM((16, 128), f32),
    ] + [pltpu.VMEM((hidden, rows_y * depth), bf16)] * 4
    per_plane = 2 * rows_y * depth * hidden * (2 * comps + hidden)
    chem = pl.pallas_call(
        functools.partial(chemistry_kernel, start=planes, planes=rest),
        in_specs=[anywhere] + [whole] * 6,
        out_specs=anywhere,
        out_shape=jax.ShapeDtypeStruct((comps, rest, rows_y, depth), f32),
        scratch_shapes=[pltpu.VMEM((comps, rest, rows_y, depth), f32)] * 2
        + prepared
        + [sems((rest,)), sems((rest,))],
        compiler_params=params,
        cost_estimate=pl.CostEstimate(
            flops=rest * per_plane,
            bytes_accessed=8 * comps * rest * rows_y * depth,
            transcendentals=2 * hidden * rest * rows_y * depth,
        ),
    )(section_scores, *weights)
    tile = (comps, rows_x, rows_y, depth)
    return pl.pallas_call(
        functools.partial(section_kernel, planes=planes, places=faces),
        in_specs=[anywhere] * 5
        + [pl.BlockSpec(memory_space=pl.ANY)] * (2 + len(parts))
        + [whole] * 6,
        out_specs=anywhere,
        out_shape=jax.ShapeDtypeStruct(tile, f32),
        scratch_shapes=[
            pltpu.VMEM((comps, rows_x + 2, rows_y, depth), f32),
            pltpu.VMEM(tile, f32),
            pltpu.VMEM((3, rows_x, rows_y, depth), f32),
            pltpu.VMEM((rows_x, rows_y, depth), f32),
            pltpu.VMEM(tile, f32),
            pltpu.VMEM(tile, f32),
        ]
        + prepared
        + [pltpu.VMEM((TILE, TILE), bf16)]
        + [sems((rows_x,))] * 4
        + [sems((rest,)), sems((2,)), sems((rows_x,))]
        + [pltpu.VMEM(part.shape, f32) for part in parts]
        + [sems((len(parts),))],
        compiler_params=params,
        cost_estimate=pl.CostEstimate(
            flops=planes * per_plane,
            bytes_accessed=16 * comps * rows_x * rows_y * depth,
            transcendentals=2 * hidden * planes * rows_y * depth,
        ),
    )(
        section_scores, base_scores, velocity, diffusivity, chem, from_low_x, from_high_x,
        *parts, *weights,
    )


def solution(mesh):
    placed = (
        P(None, "gx", "gy", None),
        P(None, "gx", "gy", None),
        P(None, "gx", "gy", None),
        P("gx", "gy", None),
        P(),
        P(),
        P(),
        P(),
        P(),
        P(),
        P(),
        P(("gx", "gy"), None, None),
        P(("gx", "gy"), None),
        P(("gx", "gy")),
    )
    return jax.shard_map(
        shards, mesh=mesh, in_specs=placed, out_specs=P(None, "gx", "gy", None), check_vma=False
    )
```

```python
import functools
import math

import jax
import jax.numpy as jnp
from jax import lax
from jax.experimental import pallas as pl
from jax.experimental.pallas import tpu as pltpu
from jax.sharding import PartitionSpec as P

SB = 32

dt_step = 0.25
keep_base = 0.75
keep_section = 0.25
scale = keep_section * dt_step

TILE = 256
f32, bf16 = jnp.float32, jnp.bfloat16


def bias_column(row, width):
    return jnp.transpose(jnp.broadcast_to(row, (width, row.shape[1])))


def weight_copies(weights, held, sems):
    return [
        pltpu.make_async_copy(weight, place, sems.at[k])
        for k, (weight, place) in enumerate(zip(weights, held))
    ]


def prepare_weights(held, w1_s, b2_s, w3_s, b3_s):
    w1t, b1, _, b2, w3, b3 = held
    comps, hidden = w1t.shape
    bias = b1[...]
    high = bias.astype(bf16).astype(f32)
    middle = (bias - high).astype(bf16).astype(f32)
    low = (bias - high - middle).astype(bf16).astype(f32)
    rows = jnp.concatenate(
        [w1t[...].astype(f32), high, middle, low]
        + [jnp.zeros((128 - comps - 3, hidden), f32)],
        axis=0,
    )
    first = jnp.transpose(rows).astype(bf16)
    w1_s[...] = jnp.concatenate(
        [first, jnp.zeros((hidden, TILE - 128), bf16)], axis=1
    )
    b2_s[...] = bias_column(b2[...], 128)
    w3_s[...] = jnp.concatenate(
        [w3[...].astype(f32), jnp.zeros((16 - comps, hidden), f32)], axis=0
    ).astype(bf16)
    row = jnp.concatenate([b3[...], jnp.zeros((1, 128 - comps), f32)], axis=1)
    b3_s[...] = bias_column(row, 128)[:16]


def regression_stages(
    cells, comps, planes, rows_y, w1_s, w2, b2_s, w3_s, b3_s, first_s, second_s, accs, put
):
    total = cells.shape[0] // comps
    across = TILE // 128
    tiles = rows_y // across
    ones = jnp.ones((16 - comps, 128), f32)
    empty = jnp.zeros((TILE - 16, TILE), bf16)
    first_acc, second_acc, third_acc = accs

    def widen(column):
        return jnp.concatenate([column] * across, axis=1)

    def layer1(row0, slot, tile):
        mxu = tile % 2
        parts = []
        for k in range(across):
            part = cells[pl.ds(row0 + tile * across + k, comps, stride=total), :]
            parts.append(jnp.concatenate([part, ones], axis=0).astype(bf16))
        block = jnp.concatenate([jnp.concatenate(parts, axis=1), empty], axis=0)
        pltpu.matmul_push_rhs(block, 0, mxu)
        pltpu.matmul_acc_lhs(first_acc[mxu], w1_s[...], load_staged_rhs=0)

        def finish():
            out = pltpu.matmul_pop(first_acc[mxu])
            first_s[slot][:, pl.ds(tile * TILE, TILE)] = jnp.tanh(out).astype(bf16)

        return finish

    def layer2(slot, tile):
        mxu = tile % 2
        pltpu.matmul_push_rhs(first_s[slot][:, pl.ds(tile * TILE, TILE)], 1, mxu)
        pltpu.matmul_acc_lhs(second_acc[mxu], w2[...], load_staged_rhs=1)

        def finish():
            out = pltpu.matmul_pop(second_acc[mxu]) + widen(b2_s[...])
            second_s[slot][:, pl.ds(tile * TILE, TILE)] = jnp.tanh(out).astype(bf16)

        return finish

    def layer3(plane, slot, tile):
        mxu = tile % 2
        pltpu.matmul_push_rhs(second_s[slot][:, pl.ds(tile * TILE, TILE)], 0, mxu)
        pltpu.matmul_acc_lhs(third_acc[mxu], w3_s[...], load_staged_rhs=0)

        def finish():
            out = pltpu.matmul_pop(third_acc[mxu]) + widen(b3_s[...])
            for k in range(across):
                put(plane, tile * across + k, out[:comps, k * 128 : (k + 1) * 128])

        return finish

    def stage(one=None, two=None, three=None, beside=None):
        late = []
        for pair in range(0, tiles, 2):
            now = range(pair, min(pair + 2, tiles))
            ready = []
            if one is not None:
                ready += [layer1(*one, t) for t in now]
            for finish in late:
                finish()
            late = []
            if three is not None:
                ready += [layer3(*three, t) for t in now]
            if two is not None:
                late = [layer2(two, t) for t in now]
            for finish in ready:
                finish()
            if beside is not None:
                beside(pair // 2, (tiles + 1) // 2)
        for finish in late:
            finish()

    return stage


def accumulators(body):
    spaces = []
    for rows in (TILE, TILE, 16):
        spaces += [pltpu.ACC(mxu_id=m)((rows, TILE), f32) for m in range(2)]

    def inner(a0, a1, b0, b1, c0, c1):
        body(((a0, a1), (b0, b1), (c0, c1)))

    pl.run_scoped(inner, *spaces)


def chemistry_kernel(section, *refs, start, planes, chunk):
    weights, out, refs = refs[:6], refs[6], refs[7:]
    (cells, held, w1_s, b2_s, w3_s, b3_s, first_0, first_1, second_0, second_1), refs = (
        refs[:10],
        refs[10:],
    )
    weights_s, (load_sem, store_sem, weight_sem) = refs[:6], refs[6:]
    first_s, second_s, w2 = (first_0, first_1), (second_0, second_1), weights_s[2]
    comps, _, rows_y, _ = section.shape

    def load(k):
        return pltpu.make_async_copy(
            section.at[:, pl.ds(start + k * chunk, chunk)],
            cells.at[:, pl.ds(k * chunk, chunk)],
            load_sem.at[k],
        )

    def store(i):
        return pltpu.make_async_copy(
            held.at[:, pl.ds(i, 1)], out.at[:, pl.ds(i, 1)], store_sem.at[i]
        )

    load(0).start()
    copies = weight_copies(weights, weights_s, weight_sem)
    for copy in copies:
        copy.start()
    for k in range(1, planes // chunk):
        load(k).start()
    for copy in copies:
        copy.wait()
    prepare_weights(weights_s, w1_s, b2_s, w3_s, b3_s)
    flat = cells.reshape(comps * planes * rows_y, 128)
    held_flat = held.reshape(comps * planes * rows_y, 128)

    def put(plane, row, value):
        held_flat[pl.ds(plane * rows_y + row, comps, stride=planes * rows_y), :] = value

    def body(accs):
        stage = regression_stages(
            flat, comps, planes, rows_y, w1_s, w2, b2_s, w3_s, b3_s, first_s, second_s, accs, put
        )
        def run(i, odd):
            stage(one=(i * rows_y, odd), two=1 - odd, three=(i - 2, odd))
            store(i - 2).start()

        load(0).wait()
        stage(one=(0, 0))
        stage(one=(rows_y, 1), two=0)
        for i in range(2, chunk):
            run(i, i % 2)

        def step(k, carry):
            load(k).wait()
            for j in range(chunk):
                run(k * chunk + j, j % 2)
            return carry

        lax.fori_loop(1, planes // chunk, step, 0)
        last = planes - 1
        stage(two=last % 2, three=(last - 1, (last - 1) % 2))
        store(last - 1).start()
        stage(three=(last, last % 2))
        store(last).start()

    accumulators(body)
    for i in range(planes):
        store(i).wait()


def section_kernel(section, base, velocity, diffusivity, chem_in, from_low_x, from_high_x, *refs, planes, places, chunk):
    parts, refs = refs[: len(places)], refs[len(places) :]
    weights, out, refs = refs[:6], refs[6], refs[7:]
    (cells, base_s, vel_s, diff_s, chem_s, out_s, place_s), refs = refs[:7], refs[7:]
    (w1_s, b2_s, w3_s, b3_s, first_0, first_1, second_0, second_1), refs = refs[:8], refs[8:]
    weights_s, refs = refs[:6], refs[6:]
    (cell_sem, base_sem, vel_sem, diff_sem, chem_sem, edge_sem, store_sem), refs = (
        refs[:7],
        refs[7:],
    )
    held_parts, (part_sem, weight_sem) = refs[: len(places)], refs[len(places) :]
    first_s, second_s, w2 = (first_0, first_1), (second_0, second_1), weights_s[2]
    comps, all_planes, rows_y, depth = section.shape
    stride = (all_planes + 2) * rows_y
    slots = parts[0].shape[1] - places[0]
    count = len(places) * slots
    low_y, high_y = held_parts[1], held_parts[2]
    spray_planes = SB // rows_y
    near_chunks = planes // chunk

    def load_cells(k):
        return pltpu.make_async_copy(
            section.at[:, pl.ds(k * chunk, chunk)],
            cells.at[:, pl.ds(k * chunk + 1, chunk)],
            cell_sem.at[k],
        )

    def load_rest(k):
        some = pl.ds(k * chunk, chunk)
        return [
            pltpu.make_async_copy(base.at[:, some], base_s.at[:, some], base_sem.at[k]),
            pltpu.make_async_copy(velocity.at[:, some], vel_s.at[:, some], vel_sem.at[k]),
            pltpu.make_async_copy(diffusivity.at[some], diff_s.at[some], diff_sem.at[k]),
        ]

    def load_chem(k):
        return pltpu.make_async_copy(
            chem_in.at[:, pl.ds(k * chunk, chunk)],
            chem_s.at[:, pl.ds(planes + k * chunk, chunk)],
            chem_sem.at[k],
        )

    def store(x):
        return pltpu.make_async_copy(
            out_s.at[:, pl.ds(x, 1)], out.at[:, pl.ds(x, 1)], store_sem.at[x]
        )

    edges = [
        pltpu.make_async_copy(from_low_x, cells.at[:, 0], edge_sem.at[0]),
        pltpu.make_async_copy(from_high_x, cells.at[:, all_planes + 1], edge_sem.at[1]),
    ]
    coming = [
        pltpu.make_async_copy(part, held, part_sem.at[k])
        for k, (part, held) in enumerate(zip(parts, held_parts))
    ]

    load_cells(0).start()
    copies = weight_copies(weights, weights_s, weight_sem)
    for copy in copies:
        copy.start()
    for k in range(near_chunks):
        for copy in load_rest(near_chunks + k) + load_rest(k):
            copy.start()
        load_cells(near_chunks + k).start()
        load_chem(k).start()
        if k == 0:
            for copy in coming + edges:
                copy.start()
        if k + 1 < near_chunks:
            load_cells(k + 1).start()
    for copy in copies:
        copy.wait()
    prepare_weights(weights_s, w1_s, b2_s, w3_s, b3_s)

    flat = cells.reshape(comps * stride, 128)
    chem_flat = chem_s.reshape(comps * all_planes * rows_y, 128)

    def put(plane, row, value):
        chem_flat[pl.ds(plane * rows_y + row, comps, stride=all_planes * rows_y), :] = value

    row_id = lax.broadcasted_iota(jnp.int32, (rows_y, depth), 0)
    lane_id = lax.broadcasted_iota(jnp.int32, (rows_y, depth), 1)

    def coefficients(x):
        spread = scale * diff_s[x]
        half = [(0.5 * scale) * vel_s[d, x] for d in range(3)]
        up = [spread - h for h in half]
        down = [spread + h for h in half]
        up[2] = jnp.where(lane_id == depth - 1, 0.0, up[2])
        down[2] = jnp.where(lane_id == 0, 0.0, down[2])
        return up, down, keep_section - 6.0 * spread

    def combine(x, comp, up, down, middle):
        center = cells[comp, x + 1]
        above_y = jnp.broadcast_to(high_y[comp, pl.ds(x, 1), :], (rows_y, depth))
        below_y = jnp.broadcast_to(low_y[comp, pl.ds(x, 1), :], (rows_y, depth))
        plus_y = jnp.where(row_id == rows_y - 1, above_y, pltpu.roll(center, rows_y - 1, 0))
        minus_y = jnp.where(row_id == 0, below_y, pltpu.roll(center, 1, 0))
        total = keep_base * base_s[comp, x] + middle * center
        total += up[0] * cells[comp, x + 2] + down[0] * cells[comp, x]
        total += up[1] * plus_y + down[1] * minus_y
        total += up[2] * pltpu.roll(center, depth - 1, 1) + down[2] * pltpu.roll(center, 1, 1)
        out_s[comp, x] = total + scale * chem_s[comp, x]

    def update(x, part=0, pieces=1):
        up, down, middle = coefficients(x)
        for comp in range(part * comps // pieces, (part + 1) * comps // pieces):
            combine(x, comp, up, down, middle)

    def deposit(first_acc):
        tags = jnp.concatenate(
            [held[comps, pl.ds(row, slots)] for held, row in zip(held_parts, places)], axis=0
        )
        lanes = lax.broadcasted_iota(jnp.int32, tags.shape, 1).astype(f32)
        chosen = jnp.transpose((tags - 1.0 == lanes).astype(f32))
        place_s[...] = jnp.zeros(place_s.shape, bf16)
        place_s[:SB, :count] = chosen[:SB].astype(bf16)
        for comp in range(0, comps, 2):
            mxu = (comp // 2) % 2
            pair = [
                jnp.concatenate(
                    [held[comp + k, pl.ds(row, slots)] for held, row in zip(held_parts, places)],
                    axis=0,
                )
                for k in range(2)
            ]
            block = jnp.concatenate(pair, axis=1).astype(bf16)
            block = jnp.concatenate([block, jnp.zeros((TILE - count, TILE), bf16)], axis=0)
            pltpu.matmul_push_rhs(block, 0, mxu)
            pltpu.matmul_acc_lhs(first_acc[mxu], place_s[...], load_staged_rhs=0)
            mine = pltpu.matmul_pop(first_acc[mxu])[:SB]
            for k in range(2):
                piece = mine[:, k * 128 : (k + 1) * 128].reshape(spray_planes, rows_y, depth)
                base_s[comp + k, :spray_planes] += (scale / keep_base) * piece

    def body(accs):
        stage = regression_stages(
            flat, comps, planes, rows_y, w1_s, w2, b2_s, w3_s, b3_s, first_s, second_s, accs, put
        )

        def run(updates, **layers):
            def beside(part, pieces):
                for k, x in enumerate(updates):
                    if k * pieces // len(updates) == part:
                        update(x)

            stage(beside=beside, **layers)
            for x in updates:
                store(x).start()

        load_cells(0).wait()
        for i in range(chunk):
            stage(
                one=((i + 1) * rows_y, i % 2),
                two=(i + 1) % 2 if i > 0 else None,
                three=(i - 2, i % 2) if i > 1 else None,
            )
        for copy in coming + edges + load_rest(0) + load_rest(near_chunks):
            copy.wait()
        load_chem(0).wait()
        load_cells(near_chunks).wait()
        deposit(accs[0])

        def step(k, carry):
            load_cells(k).wait()
            load_cells(near_chunks + k).wait()
            load_chem(k).wait()
            for copy in load_rest(k) + load_rest(near_chunks + k):
                copy.wait()
            for j in range(chunk):
                i = k * chunk + j
                far = planes + (k - 1) * more + j + 1
                updates = [far, i - chunk + 1]
                if j == chunk - 1:
                    updates += [far + 1 + n for n in range(more - chunk)]
                run(updates, one=((i + 1) * rows_y, j % 2), two=(j + 1) % 2, three=(i - 2, j % 2))
            return carry

        more = -(-(planes - 1) // (near_chunks - 1))
        lax.fori_loop(1, near_chunks, step, 0)
        last = planes - 1
        run(
            [planes, 0, last - 2],
            two=last % 2,
            three=(last - 1, (last - 1) % 2),
        )
        run([last - 1], three=(last, last % 2))
        update(last)
        store(last).start()

    accumulators(body)
    for x in range(all_planes):
        store(x).wait()


def faces_kernel(owner, block, projected, section, low_x, high_x, *refs, shifts):
    sends, (lower, upper, sems) = refs[:-3], refs[-3:]
    comps, planes, rows_y, depth = section.shape
    edge = lower.shape[2]
    count = projected.shape[1]
    tiles_y = len(shifts)
    capacity = sends[0].shape[1]
    me = lax.axis_index("gy")
    copies = [
        pltpu.make_async_copy(section.at[:, :, pl.ds(0, edge)], lower, sems.at[0]),
        pltpu.make_async_copy(section.at[:, :, pl.ds(rows_y - edge, edge)], upper, sems.at[1]),
        pltpu.make_async_copy(section.at[:, 0], low_x, sems.at[2]),
        pltpu.make_async_copy(section.at[:, planes - 1], high_x, sems.at[3]),
    ]
    for copy in copies:
        copy.start()
    own = owner[...]
    some = -(-tiles_y // 8) * 8
    hits = (lax.broadcasted_iota(jnp.int32, (some, count), 0) == own).astype(f32)
    before = lax.broadcasted_iota(jnp.int32, (count, count), 0) < lax.broadcasted_iota(
        jnp.int32, (count, count), 1
    )
    counts = jnp.dot(
        hits.astype(bf16), before.astype(f32).astype(bf16), preferred_element_type=f32
    )
    rank = jnp.sum(counts * hits, axis=0, keepdims=True).astype(jnp.int32)
    order = jnp.zeros_like(own)
    for k, shift in enumerate(shifts):
        order = jnp.where(own == lax.rem(me + shift, tiles_y), k, order)
    slot = order * capacity + rank
    chosen = lax.broadcasted_iota(jnp.int32, (tiles_y * capacity, count), 0) == slot
    numbers = jnp.sum(
        jnp.where(chosen, (block[...] + 1).astype(f32), 0.0), axis=1, keepdims=True
    )
    numbers = jnp.broadcast_to(numbers, (tiles_y * capacity, depth))
    picked = chosen.astype(f32).astype(bf16)

    def put(comp, value):
        for k, send in enumerate(sends):
            rows = pl.ds(send.shape[1] - capacity, capacity)
            send[comp, rows] = value[k * capacity : (k + 1) * capacity]

    for comp in range(comps):
        put(comp, jnp.dot(picked, projected[comp], preferred_element_type=f32))
    put(comps, numbers)
    for copy in copies:
        copy.wait()
    for send, held, row, last in (
        (sends[1], upper, edge - 1, me == tiles_y - 1),
        (sends[2], lower, 0, me == 0),
    ):
        lines = held.reshape(comps * planes * edge, depth)
        layer = lines[pl.ds(row, comps * planes, stride=edge), :]
        layer = jnp.where(last, 0.0, layer)
        for comp in range(comps):
            send[comp, pl.ds(0, planes)] = layer[comp * planes : (comp + 1) * planes]
        send[comps, pl.ds(0, planes)] = jnp.zeros((planes, depth), f32)


def shards(
    base_scores,
    section_scores,
    velocity,
    diffusivity,
    w_first,
    b_first,
    w_second,
    b_second,
    w_third,
    b_third,
    loadings,
    parcel_species,
    parcel_owner,
    parcel_block,
):
    comps, rows_x, rows_y, depth = section_scores.shape
    hidden = w_second.shape[0]
    blocks_here = parcel_species.shape[0]
    tiles_y = lax.axis_size("gy")
    capacity = max(2, 2 * blocks_here // tiles_y)
    planes = rows_x // 2
    rest = rows_x - planes
    whole = pl.BlockSpec(memory_space=pltpu.VMEM)
    anywhere = pl.BlockSpec(memory_space=pltpu.HBM)
    sems = pltpu.SemaphoreType.DMA
    params = pltpu.CompilerParams(vmem_limit_bytes=60 * 2**20)

    projected = jnp.einsum(
        "ks,psc->kpc", loadings, parcel_species, preferred_element_type=f32
    ).astype(bf16)
    shifts = [0, 1, tiles_y - 1] + list(range(2, tiles_y - 1))
    faces = [0, rows_x, rows_x] + [0] * (tiles_y - 3)
    face_x = jax.ShapeDtypeStruct((comps, rows_y, depth), f32)
    low_x, high_x, *sends = pl.pallas_call(
        functools.partial(faces_kernel, shifts=shifts),
        in_specs=[whole] * 3 + [anywhere],
        out_specs=[whole] * (2 + tiles_y),
        out_shape=[face_x] * 2
        + [jax.ShapeDtypeStruct((comps + 1, face + capacity, depth), f32) for face in faces],
        scratch_shapes=[pltpu.VMEM((comps, rows_x, 8, depth), f32)] * 2 + [sems((4,))],
        compiler_params=params,
    )(parcel_owner.reshape(1, -1), parcel_block.reshape(1, -1), projected, section_scores)

    tiles_x = lax.axis_size("gx")
    forward = [(i, i + 1) for i in range(tiles_x - 1)]
    backward = [(target, source) for source, target in forward]
    from_low_x = lax.ppermute(high_x, "gx", forward)
    from_high_x = lax.ppermute(low_x, "gx", backward)
    parts = [sends[0]] + [
        lax.ppermute(send, "gy", [(i, (i + shift) % tiles_y) for i in range(tiles_y)])
        for send, shift in zip(sends[1:], shifts[1:])
    ]

    weights = (
        w_first.T,
        b_first.reshape(1, -1),
        w_second,
        b_second.reshape(1, -1),
        w_third,
        b_third.reshape(1, -1),
    )
    prepared = [
        pltpu.VMEM((hidden, TILE), bf16),
        pltpu.VMEM((hidden, 128), f32),
        pltpu.VMEM((16, hidden), bf16),
        pltpu.VMEM((16, 128), f32),
    ] + [pltpu.VMEM((hidden, rows_y * depth), bf16)] * 4
    prepared += [pltpu.VMEM(weight.shape, weight.dtype) for weight in weights]
    chunk = math.gcd(planes, 4)
    per_plane = 2 * rows_y * depth * hidden * (2 * comps + hidden)
    chem = pl.pallas_call(
        functools.partial(chemistry_kernel, start=planes, planes=rest, chunk=chunk),
        in_specs=[anywhere] * 7,
        out_specs=anywhere,
        out_shape=jax.ShapeDtypeStruct((comps, rest, rows_y, depth), f32),
        scratch_shapes=[pltpu.VMEM((comps, rest, rows_y, depth), f32)] * 2
        + prepared
        + [sems((rest // chunk,)), sems((rest,)), sems((len(weights),))],
        compiler_params=params,
        cost_estimate=pl.CostEstimate(
            flops=rest * per_plane,
            bytes_accessed=8 * comps * rest * rows_y * depth,
            transcendentals=2 * hidden * rest * rows_y * depth,
        ),
    )(section_scores, *weights)
    tile = (comps, rows_x, rows_y, depth)
    return pl.pallas_call(
        functools.partial(section_kernel, planes=planes, places=faces, chunk=chunk),
        in_specs=[anywhere] * 5
        + [pl.BlockSpec(memory_space=pl.ANY)] * (2 + len(parts))
        + [anywhere] * 6,
        out_specs=anywhere,
        out_shape=jax.ShapeDtypeStruct(tile, f32),
        scratch_shapes=[
            pltpu.VMEM((comps, rows_x + 2, rows_y, depth), f32),
            pltpu.VMEM(tile, f32),
            pltpu.VMEM((3, rows_x, rows_y, depth), f32),
            pltpu.VMEM((rows_x, rows_y, depth), f32),
            pltpu.VMEM(tile, f32),
            pltpu.VMEM(tile, f32),
            pltpu.VMEM((TILE, TILE), bf16),
        ]
        + prepared
        + [sems((rows_x // chunk,))] * 4
        + [sems((rest // chunk,)), sems((2,)), sems((rows_x,))]
        + [pltpu.VMEM(part.shape, f32) for part in parts]
        + [sems((len(parts),)), sems((len(weights),))],
        compiler_params=params,
        cost_estimate=pl.CostEstimate(
            flops=planes * per_plane,
            bytes_accessed=16 * comps * rows_x * rows_y * depth,
            transcendentals=2 * hidden * planes * rows_y * depth,
        ),
    )(
        section_scores, base_scores, velocity, diffusivity, chem, from_low_x, from_high_x,
        *parts, *weights,
    )


def solution(mesh):
    placed = (
        P(None, "gx", "gy", None),
        P(None, "gx", "gy", None),
        P(None, "gx", "gy", None),
        P("gx", "gy", None),
        P(),
        P(),
        P(),
        P(),
        P(),
        P(),
        P(),
        P(("gx", "gy"), None, None),
        P(("gx", "gy"), None),
        P(("gx", "gy")),
    )
    return jax.shard_map(
        shards, mesh=mesh, in_specs=placed, out_specs=P(None, "gx", "gy", None), check_vma=False
    )
```

```python
import functools
import math

import jax
import jax.numpy as jnp
from jax import lax
from jax.experimental import pallas as pl
from jax.experimental.pallas import tpu as pltpu
from jax.sharding import PartitionSpec as P

SB = 32

dt_step = 0.25
keep_base = 0.75
keep_section = 0.25
scale = keep_section * dt_step

TILE = 256
f32, bf16 = jnp.float32, jnp.bfloat16


def bias_column(row, width):
    return jnp.transpose(jnp.broadcast_to(row, (width, row.shape[1])))


def weight_copies(weights, held, sems):
    return [
        pltpu.make_async_copy(weight, place, sems.at[k])
        for k, (weight, place) in enumerate(zip(weights, held))
    ]


def prepare_weights(held, w1_s, b2_s, w3_s, b3_s):
    w1t, b1, _, b2, w3, b3 = held
    comps, hidden = w1t.shape
    bias = b1[...]
    high = bias.astype(bf16).astype(f32)
    middle = (bias - high).astype(bf16).astype(f32)
    low = (bias - high - middle).astype(bf16).astype(f32)
    rows = jnp.concatenate(
        [w1t[...].astype(f32), high, middle, low]
        + [jnp.zeros((128 - comps - 3, hidden), f32)],
        axis=0,
    )
    first = jnp.transpose(rows).astype(bf16)
    w1_s[...] = jnp.concatenate(
        [first, jnp.zeros((hidden, TILE - 128), bf16)], axis=1
    )
    b2_s[...] = bias_column(b2[...], 128)
    w3_s[...] = jnp.concatenate(
        [w3[...].astype(f32), jnp.zeros((16 - comps, hidden), f32)], axis=0
    ).astype(bf16)
    row = jnp.concatenate([b3[...], jnp.zeros((1, 128 - comps), f32)], axis=1)
    b3_s[...] = bias_column(row, 128)[:16]


def regression_stages(
    cells, comps, planes, rows_y, w1_s, w2, b2_s, w3_s, b3_s, first_s, second_s, accs, put
):
    total = cells.shape[0] // comps
    across = TILE // 128
    tiles = rows_y // across
    ones = jnp.ones((16 - comps, 128), f32)
    empty = jnp.zeros((TILE - 16, TILE), bf16)
    first_acc, second_acc, third_acc = accs

    def widen(column):
        return jnp.concatenate([column] * across, axis=1)

    def layer1(row0, slot, tile):
        mxu = tile % 2
        parts = []
        for k in range(across):
            part = cells[pl.ds(row0 + tile * across + k, comps, stride=total), :]
            parts.append(jnp.concatenate([part, ones], axis=0).astype(bf16))
        block = jnp.concatenate([jnp.concatenate(parts, axis=1), empty], axis=0)
        pltpu.matmul_push_rhs(block, 0, mxu)
        pltpu.matmul_acc_lhs(first_acc[mxu], w1_s[...], load_staged_rhs=0)

        def finish():
            out = pltpu.matmul_pop(first_acc[mxu])
            first_s[slot][:, pl.ds(tile * TILE, TILE)] = jnp.tanh(out).astype(bf16)

        return finish

    def layer2(slot, tile):
        mxu = tile % 2
        pltpu.matmul_push_rhs(first_s[slot][:, pl.ds(tile * TILE, TILE)], 1, mxu)
        pltpu.matmul_acc_lhs(second_acc[mxu], w2[...], load_staged_rhs=1)

        def finish():
            out = pltpu.matmul_pop(second_acc[mxu]) + widen(b2_s[...])
            second_s[slot][:, pl.ds(tile * TILE, TILE)] = jnp.tanh(out).astype(bf16)

        return finish

    def layer3(plane, slot, tile):
        mxu = tile % 2
        pltpu.matmul_push_rhs(second_s[slot][:, pl.ds(tile * TILE, TILE)], 0, mxu)
        pltpu.matmul_acc_lhs(third_acc[mxu], w3_s[...], load_staged_rhs=0)

        def finish():
            out = pltpu.matmul_pop(third_acc[mxu]) + widen(b3_s[...])
            for k in range(across):
                put(plane, tile * across + k, out[:comps, k * 128 : (k + 1) * 128])

        return finish

    def stage(one=None, two=None, three=None, beside=None):
        late = []
        for pair in range(0, tiles, 2):
            now = range(pair, min(pair + 2, tiles))
            ready = []
            if one is not None:
                ready += [layer1(*one, t) for t in now]
            for finish in late:
                finish()
            late = []
            if three is not None:
                ready += [layer3(*three, t) for t in now]
            if two is not None:
                late = [layer2(two, t) for t in now]
            for finish in ready:
                finish()
            if beside is not None:
                beside(pair // 2, (tiles + 1) // 2)
        for finish in late:
            finish()

    return stage


def accumulators(body):
    spaces = []
    for rows in (TILE, TILE, 16):
        spaces += [pltpu.ACC(mxu_id=m)((rows, TILE), f32) for m in range(2)]

    def inner(a0, a1, b0, b1, c0, c1):
        body(((a0, a1), (b0, b1), (c0, c1)))

    pl.run_scoped(inner, *spaces)


def chemistry_kernel(section, *refs, start, planes, chunk):
    weights, out, refs = refs[:6], refs[6], refs[7:]
    (cells, held, w1_s, b2_s, w3_s, b3_s, first_0, first_1, second_0, second_1), refs = (
        refs[:10],
        refs[10:],
    )
    weights_s, (load_sem, store_sem, weight_sem) = refs[:6], refs[6:]
    first_s, second_s, w2 = (first_0, first_1), (second_0, second_1), weights_s[2]
    comps, _, rows_y, _ = section.shape

    def load(k):
        return pltpu.make_async_copy(
            section.at[:, pl.ds(start + k * chunk, chunk)],
            cells.at[:, pl.ds(k * chunk, chunk)],
            load_sem.at[k],
        )

    def store(i, some):
        return pltpu.make_async_copy(
            held.at[:, pl.ds(i, some)], out.at[:, pl.ds(i, some)], store_sem.at[i]
        )

    load(0).start()
    copies = weight_copies(weights, weights_s, weight_sem)
    for copy in copies:
        copy.start()
    for k in range(1, planes // chunk):
        load(k).start()
    for copy in copies:
        copy.wait()
    prepare_weights(weights_s, w1_s, b2_s, w3_s, b3_s)
    flat = cells.reshape(comps * planes * rows_y, 128)
    held_flat = held.reshape(comps * planes * rows_y, 128)

    def put(plane, row, value):
        held_flat[pl.ds(plane * rows_y + row, comps, stride=planes * rows_y), :] = value

    def body(accs):
        stage = regression_stages(
            flat, comps, planes, rows_y, w1_s, w2, b2_s, w3_s, b3_s, first_s, second_s, accs, put
        )
        def run(i, odd):
            stage(one=(i * rows_y, odd), two=1 - odd, three=(i - 2, odd))

        load(0).wait()
        stage(one=(0, 0))
        stage(one=(rows_y, 1), two=0)
        for i in range(2, chunk):
            run(i, i % 2)

        def step(k, carry):
            load(k).wait()
            for j in range(chunk):
                run(k * chunk + j, j % 2)
            store((k - 1) * chunk, chunk).start()
            return carry

        lax.fori_loop(1, planes // chunk, step, 0)
        last = planes - 1
        store(planes - chunk, chunk - 2).start()
        stage(two=last % 2, three=(last - 1, (last - 1) % 2))
        stage(three=(last, last % 2))
        store(last - 1, 2).start()

    accumulators(body)
    for k in range(1, planes // chunk):
        store((k - 1) * chunk, chunk).wait()
    store(planes - chunk, chunk - 2).wait()
    store(planes - 2, 2).wait()


def section_kernel(section, base, velocity, diffusivity, chem_in, from_low_x, from_high_x, *refs, planes, places, chunk):
    parts, refs = refs[: len(places)], refs[len(places) :]
    weights, out, refs = refs[:6], refs[6], refs[7:]
    (cells, base_s, vel_s, diff_s, chem_s, out_s, place_s), refs = refs[:7], refs[7:]
    (w1_s, b2_s, w3_s, b3_s, first_0, first_1, second_0, second_1), refs = refs[:8], refs[8:]
    weights_s, refs = refs[:6], refs[6:]
    (cell_sem, base_sem, vel_sem, diff_sem, chem_sem, edge_sem, store_sem), refs = (
        refs[:7],
        refs[7:],
    )
    held_parts, (part_sem, weight_sem) = refs[: len(places)], refs[len(places) :]
    first_s, second_s, w2 = (first_0, first_1), (second_0, second_1), weights_s[2]
    comps, all_planes, rows_y, depth = section.shape
    stride = (all_planes + 2) * rows_y
    slots = parts[0].shape[1] - places[0]
    count = len(places) * slots
    low_y, high_y = held_parts[1], held_parts[2]
    spray_planes = SB // rows_y
    near_chunks = planes // chunk

    def load_cells(k):
        return pltpu.make_async_copy(
            section.at[:, pl.ds(k * chunk, chunk)],
            cells.at[:, pl.ds(k * chunk + 1, chunk)],
            cell_sem.at[k],
        )

    def load_rest(k):
        some = pl.ds(k * chunk, chunk)
        return [
            pltpu.make_async_copy(base.at[:, some], base_s.at[:, some], base_sem.at[k]),
            pltpu.make_async_copy(velocity.at[:, some], vel_s.at[:, some], vel_sem.at[k]),
            pltpu.make_async_copy(diffusivity.at[some], diff_s.at[some], diff_sem.at[k]),
        ]

    def load_chem(k):
        return pltpu.make_async_copy(
            chem_in.at[:, pl.ds(k * chunk, chunk)],
            chem_s.at[:, pl.ds(planes + k * chunk, chunk)],
            chem_sem.at[k],
        )

    def store(x, some=1):
        return pltpu.make_async_copy(
            out_s.at[:, pl.ds(x, some)], out.at[:, pl.ds(x, some)], store_sem.at[x]
        )

    more = -(-(planes - 1) // (near_chunks - 1))

    def loop_stores(k):
        return [
            store((k - 1) * chunk + 1, chunk),
            store(planes + (k - 1) * more + 1, more),
        ]

    edges = [
        pltpu.make_async_copy(from_low_x, cells.at[:, 0], edge_sem.at[0]),
        pltpu.make_async_copy(from_high_x, cells.at[:, all_planes + 1], edge_sem.at[1]),
    ]
    coming = [
        pltpu.make_async_copy(part, held, part_sem.at[k])
        for k, (part, held) in enumerate(zip(parts, held_parts))
    ]

    load_cells(0).start()
    copies = weight_copies(weights, weights_s, weight_sem)
    for copy in copies:
        copy.start()
    for k in range(near_chunks):
        for copy in load_rest(near_chunks + k) + load_rest(k):
            copy.start()
        load_cells(near_chunks + k).start()
        load_chem(k).start()
        if k == 0:
            for copy in coming + edges:
                copy.start()
        if k + 1 < near_chunks:
            load_cells(k + 1).start()
    for copy in copies:
        copy.wait()
    prepare_weights(weights_s, w1_s, b2_s, w3_s, b3_s)

    flat = cells.reshape(comps * stride, 128)
    chem_flat = chem_s.reshape(comps * all_planes * rows_y, 128)

    def put(plane, row, value):
        chem_flat[pl.ds(plane * rows_y + row, comps, stride=all_planes * rows_y), :] = value

    row_id = lax.broadcasted_iota(jnp.int32, (rows_y, depth), 0)
    lane_id = lax.broadcasted_iota(jnp.int32, (rows_y, depth), 1)

    def coefficients(x):
        spread = scale * diff_s[x]
        half = [(0.5 * scale) * vel_s[d, x] for d in range(3)]
        up = [spread - h for h in half]
        down = [spread + h for h in half]
        up[2] = jnp.where(lane_id == depth - 1, 0.0, up[2])
        down[2] = jnp.where(lane_id == 0, 0.0, down[2])
        return up, down, keep_section - 6.0 * spread

    def combine(x, comp, up, down, middle):
        center = cells[comp, x + 1]
        above_y = jnp.broadcast_to(high_y[comp, pl.ds(x, 1), :], (rows_y, depth))
        below_y = jnp.broadcast_to(low_y[comp, pl.ds(x, 1), :], (rows_y, depth))
        plus_y = jnp.where(row_id == rows_y - 1, above_y, pltpu.roll(center, rows_y - 1, 0))
        minus_y = jnp.where(row_id == 0, below_y, pltpu.roll(center, 1, 0))
        total = keep_base * base_s[comp, x] + middle * center
        total += up[0] * cells[comp, x + 2] + down[0] * cells[comp, x]
        total += up[1] * plus_y + down[1] * minus_y
        total += up[2] * pltpu.roll(center, depth - 1, 1) + down[2] * pltpu.roll(center, 1, 1)
        out_s[comp, x] = total + scale * chem_s[comp, x]

    def update(x, part=0, pieces=1):
        up, down, middle = coefficients(x)
        for comp in range(part * comps // pieces, (part + 1) * comps // pieces):
            combine(x, comp, up, down, middle)

    def deposit(first_acc):
        tags = jnp.concatenate(
            [held[comps, pl.ds(row, slots)] for held, row in zip(held_parts, places)], axis=0
        )
        lanes = lax.broadcasted_iota(jnp.int32, tags.shape, 1).astype(f32)
        chosen = jnp.transpose((tags - 1.0 == lanes).astype(f32))
        place_s[...] = jnp.zeros(place_s.shape, bf16)
        place_s[:SB, :count] = chosen[:SB].astype(bf16)
        for comp in range(0, comps, 2):
            mxu = (comp // 2) % 2
            pair = [
                jnp.concatenate(
                    [held[comp + k, pl.ds(row, slots)] for held, row in zip(held_parts, places)],
                    axis=0,
                )
                for k in range(2)
            ]
            block = jnp.concatenate(pair, axis=1).astype(bf16)
            block = jnp.concatenate([block, jnp.zeros((TILE - count, TILE), bf16)], axis=0)
            pltpu.matmul_push_rhs(block, 0, mxu)
            pltpu.matmul_acc_lhs(first_acc[mxu], place_s[...], load_staged_rhs=0)
            mine = pltpu.matmul_pop(first_acc[mxu])[:SB]
            for k in range(2):
                piece = mine[:, k * 128 : (k + 1) * 128].reshape(spray_planes, rows_y, depth)
                base_s[comp + k, :spray_planes] += (scale / keep_base) * piece

    def body(accs):
        stage = regression_stages(
            flat, comps, planes, rows_y, w1_s, w2, b2_s, w3_s, b3_s, first_s, second_s, accs, put
        )

        def run(updates, **layers):
            def beside(part, pieces):
                for k, x in enumerate(updates):
                    if k * pieces // len(updates) == part:
                        update(x)

            stage(beside=beside, **layers)

        load_cells(0).wait()
        for i in range(chunk):
            stage(
                one=((i + 1) * rows_y, i % 2),
                two=(i + 1) % 2 if i > 0 else None,
                three=(i - 2, i % 2) if i > 1 else None,
            )
        for copy in coming + edges + load_rest(0) + load_rest(near_chunks):
            copy.wait()
        load_chem(0).wait()
        load_cells(near_chunks).wait()
        deposit(accs[0])

        def step(k, carry):
            load_cells(k).wait()
            load_cells(near_chunks + k).wait()
            load_chem(k).wait()
            for copy in load_rest(k) + load_rest(near_chunks + k):
                copy.wait()
            for j in range(chunk):
                i = k * chunk + j
                far = planes + (k - 1) * more + j + 1
                updates = [far, i - chunk + 1]
                if j == chunk - 1:
                    updates += [far + 1 + n for n in range(more - chunk)]
                run(updates, one=((i + 1) * rows_y, j % 2), two=(j + 1) % 2, three=(i - 2, j % 2))
            for copy in loop_stores(k):
                copy.start()
            return carry

        lax.fori_loop(1, near_chunks, step, 0)
        last = planes - 1
        run(
            [planes, 0, last - 2],
            two=last % 2,
            three=(last - 1, (last - 1) % 2),
        )
        run([last - 1], three=(last, last % 2))
        for x in (planes, 0, last - 2, last - 1):
            store(x).start()
        update(last)
        store(last).start()

    accumulators(body)
    for k in range(1, near_chunks):
        for copy in loop_stores(k):
            copy.wait()
    for x in (planes, 0, planes - 3, planes - 2, planes - 1):
        store(x).wait()


def faces_kernel(owner, block, projected, section, low_x, high_x, *refs, shifts):
    sends, (lower, upper, sems) = refs[:-3], refs[-3:]
    comps, planes, rows_y, depth = section.shape
    edge = lower.shape[2]
    count = projected.shape[1]
    tiles_y = len(shifts)
    capacity = sends[0].shape[1]
    me = lax.axis_index("gy")
    copies = [
        pltpu.make_async_copy(section.at[:, :, pl.ds(0, edge)], lower, sems.at[0]),
        pltpu.make_async_copy(section.at[:, :, pl.ds(rows_y - edge, edge)], upper, sems.at[1]),
        pltpu.make_async_copy(section.at[:, 0], low_x, sems.at[2]),
        pltpu.make_async_copy(section.at[:, planes - 1], high_x, sems.at[3]),
    ]
    for copy in copies:
        copy.start()
    own = owner[...]
    some = -(-tiles_y // 8) * 8
    hits = (lax.broadcasted_iota(jnp.int32, (some, count), 0) == own).astype(f32)
    before = lax.broadcasted_iota(jnp.int32, (count, count), 0) < lax.broadcasted_iota(
        jnp.int32, (count, count), 1
    )
    counts = jnp.dot(
        hits.astype(bf16), before.astype(f32).astype(bf16), preferred_element_type=f32
    )
    rank = jnp.sum(counts * hits, axis=0, keepdims=True).astype(jnp.int32)
    order = jnp.zeros_like(own)
    for k, shift in enumerate(shifts):
        order = jnp.where(own == lax.rem(me + shift, tiles_y), k, order)
    slot = order * capacity + rank
    chosen = lax.broadcasted_iota(jnp.int32, (tiles_y * capacity, count), 0) == slot
    numbers = jnp.sum(
        jnp.where(chosen, (block[...] + 1).astype(f32), 0.0), axis=1, keepdims=True
    )
    numbers = jnp.broadcast_to(numbers, (tiles_y * capacity, depth))
    picked = chosen.astype(f32).astype(bf16)

    def put(comp, value):
        for k, send in enumerate(sends):
            rows = pl.ds(send.shape[1] - capacity, capacity)
            send[comp, rows] = value[k * capacity : (k + 1) * capacity]

    for comp in range(comps):
        put(comp, jnp.dot(picked, projected[comp], preferred_element_type=f32))
    put(comps, numbers)
    for copy in copies:
        copy.wait()
    for send, held, row, last in (
        (sends[1], upper, edge - 1, me == tiles_y - 1),
        (sends[2], lower, 0, me == 0),
    ):
        lines = held.reshape(comps * planes * edge, depth)
        layer = lines[pl.ds(row, comps * planes, stride=edge), :]
        layer = jnp.where(last, 0.0, layer)
        for comp in range(comps):
            send[comp, pl.ds(0, planes)] = layer[comp * planes : (comp + 1) * planes]
        send[comps, pl.ds(0, planes)] = jnp.zeros((planes, depth), f32)


def shards(
    base_scores,
    section_scores,
    velocity,
    diffusivity,
    w_first,
    b_first,
    w_second,
    b_second,
    w_third,
    b_third,
    loadings,
    parcel_species,
    parcel_owner,
    parcel_block,
):
    comps, rows_x, rows_y, depth = section_scores.shape
    hidden = w_second.shape[0]
    blocks_here = parcel_species.shape[0]
    tiles_y = lax.axis_size("gy")
    capacity = max(2, 2 * blocks_here // tiles_y)
    planes = rows_x // 2
    rest = rows_x - planes
    whole = pl.BlockSpec(memory_space=pltpu.VMEM)
    anywhere = pl.BlockSpec(memory_space=pltpu.HBM)
    sems = pltpu.SemaphoreType.DMA
    params = pltpu.CompilerParams(vmem_limit_bytes=32 * 2**20)

    projected = jnp.einsum(
        "ks,psc->kpc", loadings, parcel_species, preferred_element_type=f32
    ).astype(bf16)
    shifts = [0, 1, tiles_y - 1] + list(range(2, tiles_y - 1))
    faces = [0, rows_x, rows_x] + [0] * (tiles_y - 3)
    face_x = jax.ShapeDtypeStruct((comps, rows_y, depth), f32)
    low_x, high_x, *sends = pl.pallas_call(
        functools.partial(faces_kernel, shifts=shifts),
        in_specs=[whole] * 3 + [anywhere],
        out_specs=[whole] * (2 + tiles_y),
        out_shape=[face_x] * 2
        + [jax.ShapeDtypeStruct((comps + 1, face + capacity, depth), f32) for face in faces],
        scratch_shapes=[pltpu.VMEM((comps, rows_x, 8, depth), f32)] * 2 + [sems((4,))],
        compiler_params=params,
    )(parcel_owner.reshape(1, -1), parcel_block.reshape(1, -1), projected, section_scores)

    tiles_x = lax.axis_size("gx")
    forward = [(i, i + 1) for i in range(tiles_x - 1)]
    backward = [(target, source) for source, target in forward]
    from_low_x = lax.ppermute(high_x, "gx", forward)
    from_high_x = lax.ppermute(low_x, "gx", backward)
    parts = [sends[0]] + [
        lax.ppermute(send, "gy", [(i, (i + shift) % tiles_y) for i in range(tiles_y)])
        for send, shift in zip(sends[1:], shifts[1:])
    ]

    weights = (
        w_first.T,
        b_first.reshape(1, -1),
        w_second,
        b_second.reshape(1, -1),
        w_third,
        b_third.reshape(1, -1),
    )
    prepared = [
        pltpu.VMEM((hidden, TILE), bf16),
        pltpu.VMEM((hidden, 128), f32),
        pltpu.VMEM((16, hidden), bf16),
        pltpu.VMEM((16, 128), f32),
    ] + [pltpu.VMEM((hidden, rows_y * depth), bf16)] * 4
    prepared += [pltpu.VMEM(weight.shape, weight.dtype) for weight in weights]
    chunk = math.gcd(planes, 4)
    per_plane = 2 * rows_y * depth * hidden * (2 * comps + hidden)
    chem = pl.pallas_call(
        functools.partial(chemistry_kernel, start=planes, planes=rest, chunk=chunk),
        in_specs=[anywhere] * 7,
        out_specs=anywhere,
        out_shape=jax.ShapeDtypeStruct((comps, rest, rows_y, depth), f32),
        scratch_shapes=[pltpu.VMEM((comps, rest, rows_y, depth), f32)] * 2
        + prepared
        + [sems((rest // chunk,)), sems((rest,)), sems((len(weights),))],
        compiler_params=params,
        cost_estimate=pl.CostEstimate(
            flops=rest * per_plane,
            bytes_accessed=8 * comps * rest * rows_y * depth,
            transcendentals=2 * hidden * rest * rows_y * depth,
        ),
    )(section_scores, *weights)
    tile = (comps, rows_x, rows_y, depth)
    return pl.pallas_call(
        functools.partial(section_kernel, planes=planes, places=faces, chunk=chunk),
        in_specs=[anywhere] * 5
        + [pl.BlockSpec(memory_space=pl.ANY)] * (2 + len(parts))
        + [anywhere] * 6,
        out_specs=anywhere,
        out_shape=jax.ShapeDtypeStruct(tile, f32),
        scratch_shapes=[
            pltpu.VMEM((comps, rows_x + 2, rows_y, depth), f32),
            pltpu.VMEM(tile, f32),
            pltpu.VMEM((3, rows_x, rows_y, depth), f32),
            pltpu.VMEM((rows_x, rows_y, depth), f32),
            pltpu.VMEM(tile, f32),
            pltpu.VMEM(tile, f32),
            pltpu.VMEM((TILE, TILE), bf16),
        ]
        + prepared
        + [sems((rows_x // chunk,))] * 4
        + [sems((rest // chunk,)), sems((2,)), sems((rows_x,))]
        + [pltpu.VMEM(part.shape, f32) for part in parts]
        + [sems((len(parts),)), sems((len(weights),))],
        compiler_params=params,
        cost_estimate=pl.CostEstimate(
            flops=planes * per_plane,
            bytes_accessed=16 * comps * rows_x * rows_y * depth,
            transcendentals=2 * hidden * planes * rows_y * depth,
        ),
    )(
        section_scores, base_scores, velocity, diffusivity, chem, from_low_x, from_high_x,
        *parts, *weights,
    )


def solution(mesh):
    placed = (
        P(None, "gx", "gy", None),
        P(None, "gx", "gy", None),
        P(None, "gx", "gy", None),
        P("gx", "gy", None),
        P(),
        P(),
        P(),
        P(),
        P(),
        P(),
        P(),
        P(("gx", "gy"), None, None),
        P(("gx", "gy"), None),
        P(("gx", "gy")),
    )
    return jax.shard_map(
        shards, mesh=mesh, in_specs=placed, out_specs=P(None, "gx", "gy", None), check_vma=False
    )
```

```python
import functools
import math

import jax
import jax.numpy as jnp
from jax import lax
from jax.experimental import pallas as pl
from jax.experimental.pallas import tpu as pltpu
from jax.sharding import PartitionSpec as P

SB = 32

dt_step = 0.25
keep_base = 0.75
keep_section = 0.25
scale = keep_section * dt_step

TILE = 256
f32, bf16 = jnp.float32, jnp.bfloat16


def bias_column(row, width):
    return jnp.transpose(jnp.broadcast_to(row, (width, row.shape[1])))


def weight_copies(weights, held, sems):
    return [
        pltpu.make_async_copy(weight, place, sems.at[k])
        for k, (weight, place) in enumerate(zip(weights, held))
    ]


def prepare_weights(held, w1_s, b2_s, w3_s, b3_s):
    w1t, b1, _, b2, w3, b3 = held
    comps, hidden = w1t.shape
    bias = b1[...]
    high = bias.astype(bf16).astype(f32)
    middle = (bias - high).astype(bf16).astype(f32)
    low = (bias - high - middle).astype(bf16).astype(f32)
    rows = jnp.concatenate(
        [w1t[...].astype(f32), high, middle, low]
        + [jnp.zeros((128 - comps - 3, hidden), f32)],
        axis=0,
    )
    first = jnp.transpose(rows).astype(bf16)
    w1_s[...] = jnp.concatenate(
        [first, jnp.zeros((hidden, TILE - 128), bf16)], axis=1
    )
    b2_s[...] = bias_column(b2[...], 128)
    w3_s[...] = jnp.concatenate(
        [w3[...].astype(f32), jnp.zeros((16 - comps, hidden), f32)], axis=0
    ).astype(bf16)
    row = jnp.concatenate([b3[...], jnp.zeros((1, 128 - comps), f32)], axis=1)
    b3_s[...] = bias_column(row, 128)[:16]


def regression_stages(
    cells, comps, planes, rows_y, w1_s, w2, b2_s, w3_s, b3_s, first_s, second_s, accs, put
):
    total = cells.shape[0] // comps
    across = TILE // 128
    tiles = rows_y // across
    ones = jnp.ones((16 - comps, 128), f32)
    empty = jnp.zeros((TILE - 16, TILE), bf16)
    first_acc, second_acc, third_acc = accs

    def widen(column):
        return jnp.concatenate([column] * across, axis=1)

    def layer1(row0, slot, tile):
        mxu = tile % 2
        parts = []
        for k in range(across):
            part = cells[pl.ds(row0 + tile * across + k, comps, stride=total), :]
            parts.append(jnp.concatenate([part, ones], axis=0).astype(bf16))
        block = jnp.concatenate([jnp.concatenate(parts, axis=1), empty], axis=0)
        pltpu.matmul_push_rhs(block, 0, mxu)
        pltpu.matmul_acc_lhs(first_acc[mxu], w1_s[...], load_staged_rhs=0)

        def finish():
            out = pltpu.matmul_pop(first_acc[mxu])
            first_s[slot][:, pl.ds(tile * TILE, TILE)] = jnp.tanh(out).astype(bf16)

        return finish

    def layer2(slot, tile):
        mxu = tile % 2
        pltpu.matmul_push_rhs(first_s[slot][:, pl.ds(tile * TILE, TILE)], 1, mxu)
        pltpu.matmul_acc_lhs(second_acc[mxu], w2[...], load_staged_rhs=1)

        def finish():
            out = pltpu.matmul_pop(second_acc[mxu]) + widen(b2_s[...])
            second_s[slot][:, pl.ds(tile * TILE, TILE)] = jnp.tanh(out).astype(bf16)

        return finish

    def layer3(plane, slot, tile):
        mxu = tile % 2
        pltpu.matmul_push_rhs(second_s[slot][:, pl.ds(tile * TILE, TILE)], 0, mxu)
        pltpu.matmul_acc_lhs(third_acc[mxu], w3_s[...], load_staged_rhs=0)

        def finish():
            out = pltpu.matmul_pop(third_acc[mxu]) + widen(b3_s[...])
            for k in range(across):
                put(plane, tile * across + k, out[:comps, k * 128 : (k + 1) * 128])

        return finish

    def stage(one=None, two=None, three=None, beside=None):
        late = []
        for pair in range(0, tiles, 2):
            now = range(pair, min(pair + 2, tiles))
            ready = []
            if one is not None:
                ready += [layer1(*one, t) for t in now]
            for finish in late:
                finish()
            late = []
            if three is not None:
                ready += [layer3(*three, t) for t in now]
            if two is not None:
                late = [layer2(two, t) for t in now]
            for finish in ready:
                finish()
            if beside is not None:
                beside(pair // 2, (tiles + 1) // 2)
        for finish in late:
            finish()

    return stage


def accumulators(body):
    spaces = []
    for rows in (TILE, TILE, 16):
        spaces += [pltpu.ACC(mxu_id=m)((rows, TILE), f32) for m in range(2)]

    def inner(a0, a1, b0, b1, c0, c1):
        body(((a0, a1), (b0, b1), (c0, c1)))

    pl.run_scoped(inner, *spaces)


def chemistry_kernel(section, *refs, start, planes, chunk):
    weights, out, refs = refs[:6], refs[6], refs[7:]
    (cells, held, w1_s, b2_s, w3_s, b3_s, first_0, first_1, second_0, second_1), refs = (
        refs[:10],
        refs[10:],
    )
    weights_s, (load_sem, store_sem, weight_sem) = refs[:6], refs[6:]
    first_s, second_s, w2 = (first_0, first_1), (second_0, second_1), weights_s[2]
    comps, _, rows_y, _ = section.shape

    def load(k):
        return pltpu.make_async_copy(
            section.at[:, pl.ds(start + k * chunk, chunk)],
            cells.at[:, pl.ds(k * chunk, chunk)],
            load_sem.at[k],
        )

    def store(i, some):
        return pltpu.make_async_copy(
            held.at[:, pl.ds(i, some)], out.at[:, pl.ds(i, some)], store_sem.at[i]
        )

    load(0).start()
    copies = weight_copies(weights, weights_s, weight_sem)
    for copy in copies:
        copy.start()
    for k in range(1, planes // chunk):
        load(k).start()
    for copy in copies:
        copy.wait()
    prepare_weights(weights_s, w1_s, b2_s, w3_s, b3_s)
    flat = cells.reshape(comps * planes * rows_y, 128)
    held_flat = held.reshape(comps * planes * rows_y, 128)

    def put(plane, row, value):
        held_flat[pl.ds(plane * rows_y + row, comps, stride=planes * rows_y), :] = value

    def body(accs):
        stage = regression_stages(
            flat, comps, planes, rows_y, w1_s, w2, b2_s, w3_s, b3_s, first_s, second_s, accs, put
        )
        def run(i, odd):
            stage(one=(i * rows_y, odd), two=1 - odd, three=(i - 2, odd))

        load(0).wait()
        stage(one=(0, 0))
        stage(one=(rows_y, 1), two=0)
        for i in range(2, chunk):
            run(i, i % 2)

        def step(k, carry):
            load(k).wait()
            for j in range(chunk):
                run(k * chunk + j, j % 2)
            store((k - 1) * chunk, chunk).start()
            return carry

        lax.fori_loop(1, planes // chunk, step, 0)
        last = planes - 1
        store(planes - chunk, chunk - 2).start()
        stage(two=last % 2, three=(last - 1, (last - 1) % 2))
        stage(three=(last, last % 2))
        store(last - 1, 2).start()

    accumulators(body)
    for k in range(1, planes // chunk):
        store((k - 1) * chunk, chunk).wait()
    store(planes - chunk, chunk - 2).wait()
    store(planes - 2, 2).wait()


def section_kernel(section, base, velocity, diffusivity, chem_in, from_low_x, from_high_x, *refs, planes, places, chunk):
    parts, refs = refs[: len(places)], refs[len(places) :]
    weights, out, refs = refs[:6], refs[6], refs[7:]
    (cells, base_s, vel_s, diff_s, chem_s, out_s, place_s), refs = refs[:7], refs[7:]
    (w1_s, b2_s, w3_s, b3_s, first_0, first_1, second_0, second_1), refs = refs[:8], refs[8:]
    weights_s, refs = refs[:6], refs[6:]
    (cell_sem, base_sem, vel_sem, diff_sem, chem_sem, edge_sem, store_sem), refs = (
        refs[:7],
        refs[7:],
    )
    held_parts, (part_sem, weight_sem) = refs[: len(places)], refs[len(places) :]
    first_s, second_s, w2 = (first_0, first_1), (second_0, second_1), weights_s[2]
    comps, all_planes, rows_y, depth = section.shape
    stride = (all_planes + 2) * rows_y
    slots = parts[0].shape[1] - places[0]
    count = len(places) * slots
    low_y, high_y = held_parts[1], held_parts[2]
    spray_planes = SB // rows_y
    near_chunks = planes // chunk

    def load_cells(k):
        return pltpu.make_async_copy(
            section.at[:, pl.ds(k * chunk, chunk)],
            cells.at[:, pl.ds(k * chunk + 1, chunk)],
            cell_sem.at[k],
        )

    def load_rest(k):
        some = pl.ds(k * chunk, chunk)
        return [
            pltpu.make_async_copy(base.at[:, some], base_s.at[:, some], base_sem.at[k]),
            pltpu.make_async_copy(velocity.at[:, some], vel_s.at[:, some], vel_sem.at[k]),
            pltpu.make_async_copy(diffusivity.at[some], diff_s.at[some], diff_sem.at[k]),
        ]

    def load_chem(k):
        return pltpu.make_async_copy(
            chem_in.at[:, pl.ds(k * chunk, chunk)],
            chem_s.at[:, pl.ds(planes + k * chunk, chunk)],
            chem_sem.at[k],
        )

    def store(x, some=1):
        return pltpu.make_async_copy(
            out_s.at[:, pl.ds(x, some)], out.at[:, pl.ds(x, some)], store_sem.at[x]
        )

    more = -(-(planes - 1) // (near_chunks - 1))

    def loop_stores(k):
        return [
            store((k - 1) * chunk + 1, chunk),
            store(planes + (k - 1) * more + 1, more),
        ]

    edges = [
        pltpu.make_async_copy(from_low_x, cells.at[:, 0], edge_sem.at[0]),
        pltpu.make_async_copy(from_high_x, cells.at[:, all_planes + 1], edge_sem.at[1]),
    ]
    coming = [
        pltpu.make_async_copy(part, held, part_sem.at[k])
        for k, (part, held) in enumerate(zip(parts, held_parts))
    ]

    load_cells(0).start()
    copies = weight_copies(weights, weights_s, weight_sem)
    for copy in copies:
        copy.start()
    for k in range(near_chunks):
        for copy in load_rest(near_chunks + k) + load_rest(k):
            copy.start()
        load_cells(near_chunks + k).start()
        load_chem(k).start()
        if k == 0:
            for copy in coming + edges:
                copy.start()
        if k + 1 < near_chunks:
            load_cells(k + 1).start()
    for copy in copies:
        copy.wait()
    prepare_weights(weights_s, w1_s, b2_s, w3_s, b3_s)

    flat = cells.reshape(comps * stride, 128)
    chem_flat = chem_s.reshape(comps * all_planes * rows_y, 128)

    def put(plane, row, value):
        chem_flat[pl.ds(plane * rows_y + row, comps, stride=all_planes * rows_y), :] = value

    row_id = lax.broadcasted_iota(jnp.int32, (rows_y, depth), 0)
    lane_id = lax.broadcasted_iota(jnp.int32, (rows_y, depth), 1)

    def coefficients(x):
        spread = scale * diff_s[x]
        half = [(0.5 * scale) * vel_s[d, x] for d in range(3)]
        up = [spread - h for h in half]
        down = [spread + h for h in half]
        up[2] = jnp.where(lane_id == depth - 1, 0.0, up[2])
        down[2] = jnp.where(lane_id == 0, 0.0, down[2])
        return up, down, keep_section - 6.0 * spread

    def combine(x, comp, up, down, middle):
        center = cells[comp, x + 1]
        above_y = jnp.broadcast_to(high_y[comp, pl.ds(x, 1), :], (rows_y, depth))
        below_y = jnp.broadcast_to(low_y[comp, pl.ds(x, 1), :], (rows_y, depth))
        plus_y = jnp.where(row_id == rows_y - 1, above_y, pltpu.roll(center, rows_y - 1, 0))
        minus_y = jnp.where(row_id == 0, below_y, pltpu.roll(center, 1, 0))
        total = keep_base * base_s[comp, x] + middle * center
        total += up[0] * cells[comp, x + 2] + down[0] * cells[comp, x]
        total += up[1] * plus_y + down[1] * minus_y
        total += up[2] * pltpu.roll(center, depth - 1, 1) + down[2] * pltpu.roll(center, 1, 1)
        out_s[comp, x] = total + scale * chem_s[comp, x]

    def update(x, part=0, pieces=1):
        up, down, middle = coefficients(x)
        for comp in range(part * comps // pieces, (part + 1) * comps // pieces):
            combine(x, comp, up, down, middle)

    def deposit(first_acc):
        tags = jnp.concatenate(
            [held[comps, pl.ds(row, slots)] for held, row in zip(held_parts, places)], axis=0
        )
        lanes = lax.broadcasted_iota(jnp.int32, tags.shape, 1).astype(f32)
        chosen = jnp.transpose((tags - 1.0 == lanes).astype(f32))
        place_s[...] = jnp.zeros(place_s.shape, bf16)
        place_s[:SB, :count] = chosen[:SB].astype(bf16)
        for comp in range(0, comps, 2):
            mxu = (comp // 2) % 2
            pair = [
                jnp.concatenate(
                    [held[comp + k, pl.ds(row, slots)] for held, row in zip(held_parts, places)],
                    axis=0,
                )
                for k in range(2)
            ]
            block = jnp.concatenate(pair, axis=1).astype(bf16)
            block = jnp.concatenate([block, jnp.zeros((TILE - count, TILE), bf16)], axis=0)
            pltpu.matmul_push_rhs(block, 0, mxu)
            pltpu.matmul_acc_lhs(first_acc[mxu], place_s[...], load_staged_rhs=0)
            mine = pltpu.matmul_pop(first_acc[mxu])[:SB]
            for k in range(2):
                piece = mine[:, k * 128 : (k + 1) * 128].reshape(spray_planes, rows_y, depth)
                base_s[comp + k, :spray_planes] += (scale / keep_base) * piece

    def body(accs):
        stage = regression_stages(
            flat, comps, planes, rows_y, w1_s, w2, b2_s, w3_s, b3_s, first_s, second_s, accs, put
        )

        def run(updates, **layers):
            def beside(part, pieces):
                for k, x in enumerate(updates):
                    if k * pieces // len(updates) == part:
                        update(x)

            stage(beside=beside, **layers)

        load_cells(0).wait()
        for i in range(chunk):
            stage(
                one=((i + 1) * rows_y, i % 2),
                two=(i + 1) % 2 if i > 0 else None,
                three=(i - 2, i % 2) if i > 1 else None,
            )
        for copy in coming + edges + load_rest(0) + load_rest(near_chunks):
            copy.wait()
        load_chem(0).wait()
        load_cells(near_chunks).wait()
        deposit(accs[0])

        def step(k, carry):
            load_cells(k).wait()
            load_cells(near_chunks + k).wait()
            load_chem(k).wait()
            for copy in load_rest(k) + load_rest(near_chunks + k):
                copy.wait()
            for j in range(chunk):
                i = k * chunk + j
                far = planes + (k - 1) * more + j + 1
                updates = [far, i - chunk + 1]
                if j == chunk - 1:
                    updates += [far + 1 + n for n in range(more - chunk)]
                run(updates, one=((i + 1) * rows_y, j % 2), two=(j + 1) % 2, three=(i - 2, j % 2))
            for copy in loop_stores(k):
                copy.start()
            return carry

        lax.fori_loop(1, near_chunks, step, 0)
        last = planes - 1
        run(
            [planes, 0, last - 2],
            two=last % 2,
            three=(last - 1, (last - 1) % 2),
        )
        run([last - 1], three=(last, last % 2))
        for x in (planes, 0, last - 2, last - 1):
            store(x).start()
        update(last)
        store(last).start()

    accumulators(body)
    for k in range(1, near_chunks):
        for copy in loop_stores(k):
            copy.wait()
    for x in (planes, 0, planes - 3, planes - 2, planes - 1):
        store(x).wait()


def faces_kernel(owner, block, projected, section, low_x, high_x, *refs, shifts):
    sends, (lower, upper, sems) = refs[:-3], refs[-3:]
    comps, planes, rows_y, depth = section.shape
    edge = lower.shape[2]
    count = projected.shape[1]
    tiles_y = len(shifts)
    capacity = sends[0].shape[1]
    me = lax.axis_index("gy")
    copies = [
        pltpu.make_async_copy(section.at[:, :, pl.ds(0, edge)], lower, sems.at[0]),
        pltpu.make_async_copy(section.at[:, :, pl.ds(rows_y - edge, edge)], upper, sems.at[1]),
        pltpu.make_async_copy(section.at[:, 0], low_x, sems.at[2]),
        pltpu.make_async_copy(section.at[:, planes - 1], high_x, sems.at[3]),
    ]
    for copy in copies:
        copy.start()
    own = owner[...]
    some = -(-tiles_y // 8) * 8
    hits = (lax.broadcasted_iota(jnp.int32, (some, count), 0) == own).astype(f32)
    before = lax.broadcasted_iota(jnp.int32, (count, count), 0) < lax.broadcasted_iota(
        jnp.int32, (count, count), 1
    )
    counts = jnp.dot(
        hits.astype(bf16), before.astype(f32).astype(bf16), preferred_element_type=f32
    )
    rank = jnp.sum(counts * hits, axis=0, keepdims=True).astype(jnp.int32)
    order = jnp.zeros_like(own)
    for k, shift in enumerate(shifts):
        order = jnp.where(own == lax.rem(me + shift, tiles_y), k, order)
    slot = order * capacity + rank
    chosen = lax.broadcasted_iota(jnp.int32, (tiles_y * capacity, count), 0) == slot
    numbers = jnp.sum(
        jnp.where(chosen, (block[...] + 1).astype(f32), 0.0), axis=1, keepdims=True
    )
    numbers = jnp.broadcast_to(numbers, (tiles_y * capacity, depth))
    picked = chosen.astype(f32).astype(bf16)

    def put(comp, value):
        for k, send in enumerate(sends):
            rows = pl.ds(send.shape[1] - capacity, capacity)
            send[comp, rows] = value[k * capacity : (k + 1) * capacity]

    for comp in range(comps):
        put(comp, jnp.dot(picked, projected[comp], preferred_element_type=f32))
    put(comps, numbers)
    for copy in copies:
        copy.wait()
    for send, held, row, last in (
        (sends[1], upper, edge - 1, me == tiles_y - 1),
        (sends[2], lower, 0, me == 0),
    ):
        lines = held.reshape(comps * planes * edge, depth)
        layer = lines[pl.ds(row, comps * planes, stride=edge), :]
        layer = jnp.where(last, 0.0, layer)
        for comp in range(comps):
            send[comp, pl.ds(0, planes)] = layer[comp * planes : (comp + 1) * planes]
        send[comps, pl.ds(0, planes)] = jnp.zeros((planes, depth), f32)


def shards(
    base_scores,
    section_scores,
    velocity,
    diffusivity,
    w_first,
    b_first,
    w_second,
    b_second,
    w_third,
    b_third,
    loadings,
    parcel_species,
    parcel_owner,
    parcel_block,
):
    comps, rows_x, rows_y, depth = section_scores.shape
    hidden = w_second.shape[0]
    blocks_here = parcel_species.shape[0]
    tiles_y = lax.axis_size("gy")
    capacity = max(2, 2 * blocks_here // tiles_y)
    planes = rows_x // 2
    rest = rows_x - planes
    whole = pl.BlockSpec(memory_space=pltpu.VMEM)
    anywhere = pl.BlockSpec(memory_space=pltpu.HBM)
    sems = pltpu.SemaphoreType.DMA
    params = pltpu.CompilerParams(vmem_limit_bytes=32 * 2**20)

    projected = jnp.einsum(
        "ks,psc->kpc", loadings, parcel_species, preferred_element_type=f32
    ).astype(bf16)
    shifts = [0, 1, tiles_y - 1] + list(range(2, tiles_y - 1))
    faces = [0, rows_x, rows_x] + [0] * (tiles_y - 3)
    face_x = jax.ShapeDtypeStruct((comps, rows_y, depth), f32)
    low_x, high_x, *sends = pl.pallas_call(
        functools.partial(faces_kernel, shifts=shifts),
        in_specs=[whole] * 3 + [anywhere],
        out_specs=[whole] * (2 + tiles_y),
        out_shape=[face_x] * 2
        + [jax.ShapeDtypeStruct((comps + 1, face + capacity, depth), f32) for face in faces],
        scratch_shapes=[pltpu.VMEM((comps, rows_x, 8, depth), f32)] * 2 + [sems((4,))],
        compiler_params=params,
    )(parcel_owner.reshape(1, -1), parcel_block.reshape(1, -1), projected, section_scores)

    tiles_x = lax.axis_size("gx")
    forward = [(i, i + 1) for i in range(tiles_x - 1)]
    backward = [(target, source) for source, target in forward]
    from_low_x = lax.ppermute(high_x, "gx", forward)
    from_high_x = lax.ppermute(low_x, "gx", backward)
    parts = [sends[0]] + [
        lax.ppermute(send, "gy", [(i, (i + shift) % tiles_y) for i in range(tiles_y)])
        for send, shift in zip(sends[1:], shifts[1:])
    ]

    weights = (
        w_first.T,
        b_first.reshape(1, -1),
        w_second,
        b_second.reshape(1, -1),
        w_third,
        b_third.reshape(1, -1),
    )
    prepared = [
        pltpu.VMEM((hidden, TILE), bf16),
        pltpu.VMEM((hidden, 128), f32),
        pltpu.VMEM((16, hidden), bf16),
        pltpu.VMEM((16, 128), f32),
    ] + [pltpu.VMEM((hidden, rows_y * depth), bf16)] * 4
    prepared += [pltpu.VMEM(weight.shape, weight.dtype) for weight in weights]
    chunk = math.gcd(planes, 4)
    per_plane = 2 * rows_y * depth * hidden * (2 * comps + hidden)
    chem = pl.pallas_call(
        functools.partial(chemistry_kernel, start=planes, planes=rest, chunk=chunk),
        in_specs=[anywhere] * 7,
        out_specs=anywhere,
        out_shape=jax.ShapeDtypeStruct((comps, rest, rows_y, depth), f32),
        scratch_shapes=[pltpu.VMEM((comps, rest, rows_y, depth), f32)] * 2
        + prepared
        + [sems((rest // chunk,)), sems((rest,)), sems((len(weights),))],
        compiler_params=params,
        cost_estimate=pl.CostEstimate(
            flops=rest * per_plane,
            bytes_accessed=8 * comps * rest * rows_y * depth,
            transcendentals=2 * hidden * rest * rows_y * depth,
        ),
    )(section_scores, *weights)
    tile = (comps, rows_x, rows_y, depth)
    return pl.pallas_call(
        functools.partial(section_kernel, planes=planes, places=faces, chunk=chunk),
        in_specs=[anywhere]
        + [pl.BlockSpec(memory_space=pl.ANY)] * (6 + len(parts))
        + [anywhere] * 6,
        out_specs=anywhere,
        out_shape=jax.ShapeDtypeStruct(tile, f32),
        scratch_shapes=[
            pltpu.VMEM((comps, rows_x + 2, rows_y, depth), f32),
            pltpu.VMEM(tile, f32),
            pltpu.VMEM((3, rows_x, rows_y, depth), f32),
            pltpu.VMEM((rows_x, rows_y, depth), f32),
            pltpu.VMEM(tile, f32),
            pltpu.VMEM(tile, f32),
            pltpu.VMEM((TILE, TILE), bf16),
        ]
        + prepared
        + [sems((rows_x // chunk,))] * 4
        + [sems((rest // chunk,)), sems((2,)), sems((rows_x,))]
        + [pltpu.VMEM(part.shape, f32) for part in parts]
        + [sems((len(parts),)), sems((len(weights),))],
        compiler_params=params,
        cost_estimate=pl.CostEstimate(
            flops=planes * per_plane,
            bytes_accessed=16 * comps * rows_x * rows_y * depth,
            transcendentals=2 * hidden * planes * rows_y * depth,
        ),
    )(
        section_scores, base_scores, velocity, diffusivity, chem, from_low_x, from_high_x,
        *parts, *weights,
    )


def solution(mesh):
    placed = (
        P(None, "gx", "gy", None),
        P(None, "gx", "gy", None),
        P(None, "gx", "gy", None),
        P("gx", "gy", None),
        P(),
        P(),
        P(),
        P(),
        P(),
        P(),
        P(),
        P(("gx", "gy"), None, None),
        P(("gx", "gy"), None),
        P(("gx", "gy")),
    )
    return jax.shard_map(
        shards, mesh=mesh, in_specs=placed, out_specs=P(None, "gx", "gy", None), check_vma=False
    )
```
